1024 devices in a mesh: expert: 64 (over x, y_lo, core), tensor: 16 (over z, y_hi).
Axes of the slice: x: 8, y: 8 (y_hi: 2, y_lo: 4; y = y_hi * 4 + y_lo), z: 8, core: 2. Of those that a mesh axis runs over, the one named last changes fastest.
Arguments:
- out_grad: bfloat16 [16384, 3584], P('expert', 'tensor'), may hold values from -6 to 6
- router_logits: float32 [16384, 2], P('expert'), may hold values from -6 to 6
- expert_ids: int32 [16384, 2], P('expert'), may hold values from 0 to 63, as said below
- slot_ids: int32 [16384, 2], P('expert'), may hold values from 0 to 11, as said below
- down_weight: bfloat16 [64, 2432, 3584], P('expert', 'tensor'), may hold values from -0.125 to 0.125
- gate_pre: bfloat16 [64, 768, 2432], P('expert', None, 'tensor'), may hold values from -6 to 6
- up_pre: bfloat16 [64, 768, 2432], P('expert', None, 'tensor'), may hold values from -6 to 6
Outputs:
- down_grad: bfloat16 [64, 2432, 3584], P('expert', 'tensor')
- gate_grad: bfloat16 [64, 768, 2432], P('expert', None, 'tensor')
- up_grad: bfloat16 [64, 768, 2432], P('expert', None, 'tensor')
- router_grad: float32 [16384, 2], P('expert')
The draws below stay inside these ranges and needn't reach their ends.
Inputs may be any that keep to these rules, and one draw needn't show every extreme that they name: `expert_ids`: the two experts of a token differ. Within each block of 256 consecutive tokens no expert is named by more than 12 tokens, and one expert, the same in all blocks, is named by exactly 12 tokens in every block. `slot_ids`: within each block of 256 consecutive tokens, the n tokens that name an expert carry the slots 0 to n - 1 for it, each once.
All inputs are finite; a program needn't handle non-finite values.
Results may differ from the reference program's by a relative error of at most 0.0056.
Values may be sent and summed in bfloat16 or wider, within the bound.
A program may use at most 32 MiB of HBM per device.

```python
import jax
import jax.numpy as jnp
from jax import lax

D = 3584
EH = 2432
TOK_DEV = 256
EXPERTS = 64
TOKENS = 16384
CAP = 12
ROWS = 768


def block_routes(key, favored):
    subkeys = jax.random.split(key, 5)
    levels = jax.random.randint(subkeys[0], (EXPERTS,), 0, 3 * CAP)
    second = jax.random.randint(subkeys[1], (), 0, EXPERTS)
    labels = jnp.arange(EXPERTS)
    levels = jnp.where((labels == second) | (labels == favored), 4 * CAP, levels)
    slot_values = levels[:, None] - jnp.arange(CAP)[None, :] + CAP
    tiebreak = jax.random.permutation(subkeys[2], EXPERTS * CAP)
    scores = slot_values.reshape(-1) * (EXPERTS * CAP) + tiebreak
    picked = lax.top_k(scores, 2 * TOK_DEV)[1].astype(jnp.int32)
    grouped = jnp.sort(picked)
    ordering = jax.random.permutation(subkeys[3], TOK_DEV)
    leading = jnp.zeros((TOK_DEV,), jnp.int32).at[ordering].set(grouped[:TOK_DEV])
    trailing = jnp.zeros((TOK_DEV,), jnp.int32).at[ordering].set(grouped[TOK_DEV:])
    flipped = jax.random.randint(subkeys[4], (TOK_DEV,), 0, 2)
    first_col = jnp.where(flipped == 1, trailing, leading)
    second_col = jnp.where(flipped == 1, leading, trailing)
    return jnp.stack([first_col, second_col], 1)


def route_table(key):
    favored = jax.random.randint(jax.random.fold_in(key, 7), (), 0, EXPERTS)
    blocks = jax.random.split(jax.random.fold_in(key, 11), TOKENS // TOK_DEV)
    flat_ids = jax.vmap(block_routes, in_axes=(0, None))(blocks, favored).reshape(TOKENS, 2)
    return (flat_ids // CAP, flat_ids % CAP)


def draw_expert_ids(key, part):
    expert_ids, slot_ids = route_table(key)
    return expert_ids.astype(jnp.int32)


def draw_slot_ids(key, part):
    expert_ids, slot_ids = route_table(key)
    return slot_ids.astype(jnp.int32)


def level_of(key, shape, cuts, smallest, high):
    loudness = 1.0
    for axis_at, parts in cuts:
        draws = jax.random.uniform(jax.random.fold_in(jax.random.fold_in(key, 6), axis_at), (parts,), jnp.float32, smallest / len(cuts), high / len(cuts))
        loudness = loudness * jnp.repeat(jnp.exp(draws), shape[axis_at] // parts).reshape((-1,) + (1,) * (len(shape) - 1 - axis_at))
    return loudness


def centred(rng, extent, deviation, most, pieces=(), held_as=jnp.bfloat16):
    array = deviation * jax.random.normal(rng, extent, jnp.float32)
    if pieces:
        array = array * level_of(rng, extent, pieces, -0.22, 0.18)
    return jnp.clip(array, -most, most).astype(held_as)


def setup_inputs(seed: int = 0) -> dict:
    arg_keys = jax.random.split(jax.random.key(seed), 8)
    return {
        "out_grad": centred(arg_keys[0], (TOKENS, D), 1.0, 6.0, ((0, 64), (1, 16))),
        "router_logits": centred(arg_keys[1], (TOKENS, 2), 1.5, 6.0, ((0, 64),), jnp.float32),
        "expert_ids": draw_expert_ids(jax.random.fold_in(arg_keys[7], 71), 0),
        "slot_ids": draw_slot_ids(jax.random.fold_in(arg_keys[7], 71), 0),
        "down_weight": centred(arg_keys[4], (EXPERTS, EH, D), EH ** -0.5, 0.125, ((0, 64), (1, 16))),
        "gate_pre": centred(arg_keys[5], (EXPERTS, ROWS, EH), 1.0, 6.0, ((0, 64), (2, 16))),
        "up_pre": centred(arg_keys[6], (EXPERTS, ROWS, EH), 1.0, 6.0, ((0, 64), (2, 16))),
    }


def expert_backward(inputs):
    grad_rows, slot_weight, weight, gate_pre, up_pre = inputs
    gate_f = gate_pre.astype(jnp.float32)
    up_f = up_pre.astype(jnp.float32)
    sigma_gate = jax.nn.sigmoid(gate_f)
    silu_gate = gate_f * sigma_gate
    activation = silu_gate * up_f
    hidden_back = jnp.dot(grad_rows, weight.T, preferred_element_type=jnp.float32)
    row_probe = jnp.sum(hidden_back * activation, axis=1)
    hidden_grad = slot_weight[:, None] * hidden_back
    gate_grad = (hidden_grad * up_f * (sigma_gate * (1.0 + gate_f * (1.0 - sigma_gate)))).astype(jnp.bfloat16)
    up_grad = (hidden_grad * silu_gate).astype(jnp.bfloat16)
    scaled = (slot_weight[:, None] * activation).astype(jnp.bfloat16)
    down_grad = jnp.dot(scaled.T, grad_rows, preferred_element_type=jnp.float32).astype(jnp.bfloat16)
    return down_grad, gate_grad, up_grad, row_probe


def reference(out_grad, router_logits, expert_ids, slot_ids, down_weight, gate_pre, up_pre):
    gate_share = jax.nn.sigmoid(router_logits[:, 0] - router_logits[:, 1])
    combine = jnp.stack([gate_share, 1.0 - gate_share], 1).astype(jnp.bfloat16)
    source = (jnp.arange(TOKENS) // TOK_DEV).astype(jnp.int32)
    slot_row = (source[:, None] * CAP + slot_ids).astype(jnp.int32)
    received = jnp.zeros((EXPERTS, ROWS, D), out_grad.dtype)
    received = received.at[expert_ids, slot_row].set(jnp.broadcast_to(out_grad[:, None, :], (TOKENS, 2, D)))
    slot_weight = jnp.zeros((EXPERTS, ROWS), jnp.float32)
    slot_weight = slot_weight.at[expert_ids, slot_row].set(combine.astype(jnp.float32))
    down_grad, gate_grad, up_grad, row_probe = lax.map(expert_backward, (received, slot_weight, down_weight, gate_pre, up_pre))
    token_probe = row_probe[expert_ids, slot_row]
    slope = (token_probe[:, 0] - token_probe[:, 1]) * gate_share * (1.0 - gate_share)
    router_grad = jnp.stack([slope, -slope], 1)
    return down_grad, gate_grad, up_grad, router_grad
```

```python
import functools

import jax
import jax.numpy as jnp
from jax import lax
from jax.experimental import pallas as pl
from jax.experimental.pallas import tpu as pltpu
from jax.sharding import PartitionSpec as P

MESH = pl.DeviceIdType.MESH
BF16 = jnp.bfloat16
F32 = jnp.float32
LANES = 128


def dot(a, b, contract=((1,), (0,)), precision=None):
    return lax.dot_general(
        a, b, (contract, ((), ())), preferred_element_type=F32, precision=precision
    )


def iota(shape, dim):
    return lax.broadcasted_iota(jnp.int32, shape, dim)


def kernel(
    dims, og, rl, ei, si, w_hbm, gp_hbm, up_hbm, dg_hbm, gg_hbm, ug_hbm, rg,
    w, gp, up, dg, gg, ug,
    perm, ext, xs, xr, ys, yr, g, wp, dgp, hid, act, f1, f2, scaled_t,
    vz, vy, vx, vsum, usum, load_sem, store_sem,
    xsend, xrecv, ysend, yrecv, zsend, zrecv, pzsend, pzrecv, pysend, pyrecv, pxsend, pxrecv,
):
    nx, ny, nc, nz, cap = dims
    nb = ny * nc
    group = nb * cap
    rows = nx * group
    feats = og.shape[1]
    head = feats - LANES
    hidden = w.shape[0]
    e, t = lax.axis_index("expert"), lax.axis_index("tensor")
    x, b = e // nb, e % nb
    z, half = t // 2, t % 2

    def xpeer(i):
        return lax.rem(x + i, nx)

    def bpeer(i):
        return lax.rem(b + i, nb)

    def zpeer(i):
        return lax.rem(z + i + nz, nz)

    def device(x_, b_, z_, half_):
        return {"expert": x_ * nb + b_, "tensor": z_ * 2 + half_}

    def remote(src, dst, send, recv, where):
        return pltpu.make_async_remote_copy(
            src_ref=src, dst_ref=dst, send_sem=send, recv_sem=recv,
            device_id=where, device_id_type=MESH,
        )

    loads = [
        pltpu.make_async_copy(gp_hbm.at[0], gp, load_sem.at[0]),
        pltpu.make_async_copy(up_hbm.at[0], up, load_sem.at[1]),
        pltpu.make_async_copy(w_hbm.at[0], w, load_sem.at[2]),
    ]
    for copy in loads:
        copy.start()

    barrier = pltpu.get_barrier_semaphore()
    peers = [device(xpeer(i), b, z, half) for i in range(1, nx)]
    peers += [device(x, bpeer(i), z, half) for i in range(1, nb)]
    peers += [device(x, bpeer(i), z, 1 - half) for i in range(nb)]
    peers += [device(x, b, zpeer(i), half) for i in range(1, nz)]
    for peer in peers:
        pl.semaphore_signal(barrier, inc=1, device_id=peer, device_id_type=MESH)

    share = jax.nn.sigmoid(rl[:, 0:1] - rl[:, 1:2])
    combine = [share.astype(BF16), (1.0 - share).astype(BF16)]
    tokens = og.shape[0]
    outgoing = None
    for k in range(2):
        ext[k, :, 0:head] = og[:, 0:head]
        ext[k, :, LANES : 2 * LANES] = og[:, head:feats]
        ext[k, :, head:LANES] = jnp.where(
            iota((tokens, LANES - head), 1) == 0, combine[k].astype(F32), 0.0
        ).astype(BF16)
        slot = ei[:, k : k + 1] * cap + si[:, k : k + 1]
        chosen = (iota((tokens, rows), 1) == slot).astype(F32).astype(BF16)
        part = dot(chosen, ext[k], ((0,), (0,)))
        outgoing = part if outgoing is None else outgoing + part
    outgoing = outgoing.astype(BF16)
    for c in range(2):
        xs[c] = outgoing[:, c * LANES : (c + 1) * LANES].reshape(nx, group, LANES)

    pl.semaphore_wait(barrier, len(peers))

    xcopies = [
        [
            remote(xs.at[c, xpeer(i)], xr.at[c, x], xsend.at[c, i], xrecv.at[c, x],
                   device(xpeer(i), b, z, half))
            for i in range(1, nx)
        ]
        for c in range(2)
    ]
    for c in range(2):
        for copy in xcopies[c]:
            copy.start()

    i_row = iota((rows, 1), 0)
    major = i_row // (nx * cap)
    rest = i_row - major * (nx * cap)
    minor = rest // cap
    source = minor * group + major * cap + (rest - minor * cap)
    perm[...] = (iota((rows, rows), 1) == source).astype(F32).astype(BF16)

    ycopies = [[None, None], [None, None]]
    for c in range(2):
        xr[c, x] = xs[c, x]
        for i in range(1, nx):
            remote(xs.at[c, x], xr.at[c, xpeer(i)], xsend.at[c, i], xrecv.at[c, xpeer(i)],
                   device(xpeer(i), b, z, half)).wait_recv()
        turned = dot(perm[...], xr[c].reshape(rows, LANES)).astype(BF16)
        ys[c] = turned.reshape(nb, nx * cap, LANES)
        yr[0, c, b] = ys[c, b]
        ycopies[0][c] = [
            remote(ys.at[c, bpeer(i)], yr.at[0, c, b], ysend.at[0, c, i], yrecv.at[0, c, b],
                   device(x, bpeer(i), z, half))
            for i in range(1, nb)
        ]
        for copy in ycopies[0][c]:
            copy.start()
    for c in range(2):
        ycopies[1][c] = [
            remote(ys.at[c, bpeer(i)], yr.at[1, c, b], ysend.at[1, c, i], yrecv.at[1, c, b],
                   device(x, bpeer(i), z, 1 - half))
            for i in range(nb)
        ]
        for copy in ycopies[1][c]:
            copy.start()

    for copy in loads:
        copy.wait()
    for s in range(2 * nz):
        wp[s, :, 0:head] = w[:, s * feats : s * feats + head]
        wp[s, :, head:LANES] = jnp.zeros((hidden, LANES - head), BF16)
        wp[s, :, LANES : 2 * LANES] = w[:, s * feats + head : (s + 1) * feats]

    longer, shorter = nz // 2, nz - 1 - nz // 2
    hops = [(longer, shorter), (shorter, longer), (shorter, longer), (longer, shorter)]
    zcopies = []

    def zsend_start(q, src, way):
        to = zpeer(1) if way == 0 else zpeer(-1)
        copy = remote(g.at[src, q], g.at[src, q], zsend.at[way, q, src], zrecv.at[q, src],
                      device(x, b, to, half))
        copy.start()
        zcopies.append(copy)

    def zwait(q, src):
        remote(g.at[src, q], g.at[src, q], zsend.at[0, q, src], zrecv.at[q, src],
               device(x, b, zpeer(1), half)).wait_recv()

    hid[...] = jnp.zeros_like(hid)

    def work(q, src):
        h, c = q // 2, q % 2
        shard = src * 2 + (half if h == 0 else 1 - half)
        block = g[src, q]
        cols = slice(c * LANES, (c + 1) * LANES)
        hid[...] += dot(block, wp[shard, :, cols], ((1,), (1,)))
        dgp[shard, :, cols] = dot(scaled_t[...], block).astype(BF16)

    for d in range(4 + nz // 2):
        ready = []
        if d < 4:
            h, c = d // 2, d % 2
            for i in range(1 if h == 0 else 0, nb):
                remote(ys.at[c, b], yr.at[h, c, bpeer(i)], ysend.at[h, c, i],
                       yrecv.at[h, c, bpeer(i)], device(x, bpeer(i), z, half)).wait_recv()
            canon = dot(perm[...], yr[h, c].reshape(rows, LANES),
                        ((0,), (0,)) if nx != nb else ((1,), (0,)))
            g[z, d] = canon.astype(BF16)
            zsend_start(d, z, 0)
            zsend_start(d, z, 1)
            ready.append((d, z))
        for q in range(4):
            s = d - q
            if s < 1:
                continue
            for way in range(2):
                if s <= hops[q][way]:
                    src = zpeer(-s) if way == 0 else zpeer(s)
                    zwait(q, src)
                    if s < hops[q][way]:
                        zsend_start(q, src, way)
                    ready.append((q, src))
        if d == 0:
            slot_weight = g[z, 0, :, head : head + 1].astype(F32)
            gate = gp[...].astype(F32)
            upf = up[...].astype(F32)
            sigma = jax.nn.sigmoid(gate)
            silu = gate * sigma
            act[...] = silu * upf
            scaled = (slot_weight * act[...]).astype(BF16)
            scaled_t[...] = jnp.transpose(scaled)
            f1[...] = slot_weight * (upf * (sigma * (1.0 + gate * (1.0 - sigma))))
            f2[...] = slot_weight * silu
        for q, src in ready:
            work(q, src)

    probe = jnp.sum(hid[...] * act[...], axis=1, keepdims=True)
    i_row = iota((rows, 1), 0)
    i_x = i_row // group
    i_rest = i_row - i_x * group
    i_b = i_rest // cap
    i_lane = i_x * cap + (i_rest - i_b * cap)
    spread = jnp.where(iota((rows, LANES), 1) == i_lane, probe, 0.0)
    j_row = iota((1, rows), 1)
    j_rest = j_row - (j_row // group) * group
    gather = (iota((nb, rows), 0) == j_rest // cap).astype(F32)
    vz[z] = dot(gather, spread, precision=lax.Precision.HIGHEST)
    pz = [
        remote(vz.at[z], vz.at[z], pzsend.at[i], pzrecv.at[z], device(x, b, zpeer(i), half))
        for i in range(1, nz)
    ]
    for copy in pz:
        copy.start()

    gg[...] = (hid[...] * f1[...]).astype(BF16)
    ug[...] = (hid[...] * f2[...]).astype(BF16)
    stores = [
        pltpu.make_async_copy(gg, gg_hbm.at[0], store_sem.at[0]),
        pltpu.make_async_copy(ug, ug_hbm.at[0], store_sem.at[1]),
    ]
    for copy in stores:
        copy.start()

    for i in range(1, nz):
        remote(vz.at[z], vz.at[zpeer(i)], pzsend.at[i], pzrecv.at[zpeer(i)],
               device(x, b, zpeer(i), half)).wait_recv()
    vsum[...] = jnp.sum(vz[...], axis=0)
    vy[half, b] = vsum[...]
    py = [
        remote(vsum, vy.at[half, b], pysend.at[0, i], pyrecv.at[half, b],
               device(x, bpeer(i), z, half))
        for i in range(1, nb)
    ]
    py += [
        remote(vsum, vy.at[half, b], pysend.at[1, i], pyrecv.at[half, b],
               device(x, bpeer(i), z, 1 - half))
        for i in range(nb)
    ]
    for copy in py:
        copy.start()

    for s in range(2 * nz):
        dg[:, s * feats : s * feats + head] = dgp[s, :, 0:head]
        dg[:, s * feats + head : (s + 1) * feats] = dgp[s, :, LANES : 2 * LANES]
    stores.append(pltpu.make_async_copy(dg, dg_hbm.at[0], store_sem.at[2]))
    stores[-1].start()

    for i in range(1, nb):
        remote(vsum, vy.at[half, bpeer(i)], pysend.at[0, i], pyrecv.at[half, bpeer(i)],
               device(x, bpeer(i), z, half)).wait_recv()
    for i in range(nb):
        remote(vsum, vy.at[1 - half, bpeer(i)], pysend.at[1, i],
               pyrecv.at[1 - half, bpeer(i)], device(x, bpeer(i), z, 1 - half)).wait_recv()
    mine = iota((nb, LANES), 0) == b
    for i in range(nb):
        both = vy[0, i] + vy[1, i]
        usum[i : i + 1, :] = jnp.sum(jnp.where(mine, both, 0.0), axis=0, keepdims=True)
    vx[x] = usum[...]
    px = [
        remote(usum, vx.at[x], pxsend.at[i], pxrecv.at[x], device(xpeer(i), b, z, half))
        for i in range(1, nx)
    ]
    for copy in px:
        copy.start()
    for i in range(1, nx):
        remote(usum, vx.at[xpeer(i)], pxsend.at[i], pxrecv.at[xpeer(i)],
               device(xpeer(i), b, z, half)).wait_recv()
    table = vx[...].reshape(nx * nb, LANES)
    token_probe = []
    for k in range(2):
        picked = (iota((tokens, nx * nb), 1) == ei[:, k : k + 1]).astype(F32)
        found = dot(picked, table, precision=lax.Precision.HIGHEST)
        lane = x * cap + si[:, k : k + 1]
        token_probe.append(
            jnp.sum(jnp.where(iota((tokens, LANES), 1) == lane, found, 0.0), axis=1, keepdims=True)
        )
    slope = (token_probe[0] - token_probe[1]) * share * (1.0 - share)
    rg[:, 0:1] = slope
    rg[:, 1:2] = -slope

    for c in range(2):
        for copy in xcopies[c]:
            copy.wait_send()
        for h in range(2):
            for copy in ycopies[h][c]:
                copy.wait_send()
    for copy in zcopies + pz + py + px:
        copy.wait_send()
    for copy in stores:
        copy.wait()


def shards(dims, out_grad, router_logits, expert_ids, slot_ids, down_weight, gate_pre, up_pre):
    nx, ny, nc, nz, cap = dims
    nb = ny * nc
    rows = nx * nb * cap
    tokens, feats = out_grad.shape
    hidden, width = down_weight.shape[1:]
    vmem = pl.BlockSpec(memory_space=pltpu.VMEM)
    hbm = pl.BlockSpec(memory_space=pl.ANY)
    dma = pltpu.SemaphoreType.DMA
    return pl.pallas_call(
        functools.partial(kernel, dims),
        out_shape=(
            jax.ShapeDtypeStruct(down_weight.shape, BF16),
            jax.ShapeDtypeStruct(gate_pre.shape, BF16),
            jax.ShapeDtypeStruct(up_pre.shape, BF16),
            jax.ShapeDtypeStruct(router_logits.shape, F32),
        ),
        in_specs=[vmem] * 4 + [hbm] * 3,
        out_specs=(hbm, hbm, hbm, vmem),
        scratch_shapes=[
            pltpu.VMEM((hidden, width), BF16),
            pltpu.VMEM((rows, hidden), BF16),
            pltpu.VMEM((rows, hidden), BF16),
            pltpu.VMEM((hidden, width), BF16),
            pltpu.VMEM((rows, hidden), BF16),
            pltpu.VMEM((rows, hidden), BF16),
            pltpu.VMEM((rows, rows), BF16),
            pltpu.VMEM((2, tokens, 2 * LANES), BF16),
            pltpu.VMEM((2, nx, nb * cap, LANES), BF16),
            pltpu.VMEM((2, nx, nb * cap, LANES), BF16),
            pltpu.VMEM((2, nb, nx * cap, LANES), BF16),
            pltpu.VMEM((2, 2, nb, nx * cap, LANES), BF16),
            pltpu.VMEM((nz, 4, rows, LANES), BF16),
            pltpu.VMEM((2 * nz, hidden, 2 * LANES), BF16),
            pltpu.VMEM((2 * nz, hidden, 2 * LANES), BF16),
            pltpu.VMEM((rows, hidden), F32),
            pltpu.VMEM((rows, hidden), F32),
            pltpu.VMEM((rows, hidden), F32),
            pltpu.VMEM((rows, hidden), F32),
            pltpu.VMEM((hidden, rows), BF16),
            pltpu.VMEM((nz, nb, LANES), F32),
            pltpu.VMEM((2, nb, nb, LANES), F32),
            pltpu.VMEM((nx, nb, LANES), F32),
            pltpu.VMEM((nb, LANES), F32),
            pltpu.VMEM((nb, LANES), F32),
            dma((3,)),
            dma((3,)),
            dma((2, nx)),
            dma((2, nx)),
            dma((2, 2, nb)),
            dma((2, 2, nb)),
            dma((2, 4, nz)),
            dma((4, nz)),
            dma((nz,)),
            dma((nz,)),
            dma((2, nb)),
            dma((2, nb)),
            dma((nx,)),
            dma((nx,)),
        ],
        compiler_params=pltpu.CompilerParams(
            collective_id=0, has_side_effects=True, vmem_limit_bytes=48 * 1024 * 1024
        ),
    )(out_grad, router_logits, expert_ids, slot_ids, down_weight, gate_pre, up_pre)


def solution(mesh, dims=(8, 4, 2, 8, 12)):
    placed = (
        P("expert", "tensor"),
        P("expert", None),
        P("expert", None),
        P("expert", None),
        P("expert", "tensor", None),
        P("expert", None, "tensor"),
        P("expert", None, "tensor"),
    )
    return jax.shard_map(
        functools.partial(shards, dims),
        mesh=mesh,
        in_specs=placed,
        out_specs=(
            P("expert", "tensor", None),
            P("expert", None, "tensor"),
            P("expert", None, "tensor"),
            P("expert", None),
        ),
        check_vma=False,
    )
```

```python
import contextlib
import functools

import jax
import jax.numpy as jnp
from jax import lax
from jax.experimental import pallas as pl
from jax.experimental.pallas import tpu as pltpu
from jax.sharding import PartitionSpec as P

MESH = pl.DeviceIdType.MESH
BF16 = jnp.bfloat16
F32 = jnp.float32
LANES = 128
VMEM_BYTES = 62 * 1024 * 1024


def dot(a, b, contract=((1,), (0,)), precision=None):
    return lax.dot_general(
        a, b, (contract, ((), ())), preferred_element_type=F32, precision=precision
    )


def iota(shape, dim):
    return lax.broadcasted_iota(jnp.int32, shape, dim)


def scope(name):
    return contextlib.nullcontext()


def kernel(
    dims, og_hbm, rl_hbm, ei_hbm, si_hbm, w_hbm, gp_hbm, up_hbm,
    dg_hbm, gg_hbm, ug_hbm, rg_hbm,
    og, rl, ei, si, w, gp, up, dg, gg, ug, rg,
    perm, spread, ext, xs, xr, ys, yr, g0, g1, unpacked, sw, wp, dgp, hid, act, f1, f2, scaled_t,
    vz, vy, vx, vsum, usum, load_sem, store_sem,
    xsend, xrecv, ysend, yrecv, zsend, zrecv, pzsend, pzrecv, pysend, pyrecv, pxsend, pxrecv,
):
    nx, ny, nc, nz, cap = dims
    nb = ny * nc
    group = nb * cap
    rows = nx * group
    feats = og.shape[0]
    head = feats - LANES
    hidden = w.shape[0]
    e, t = lax.axis_index("expert"), lax.axis_index("tensor")
    x, b = e // nb, e % nb
    z, half = t // 2, t % 2

    def xpeer(i):
        return lax.rem(x + i, nx)

    def bpeer(i):
        return lax.rem(b + i, nb)

    def zpeer(i):
        return lax.rem(z + i + nz, nz)

    def device(x_, b_, z_, half_):
        return {"expert": x_ * nb + b_, "tensor": z_ * 2 + half_}

    def remote(src, dst, send, recv, where):
        return pltpu.make_async_remote_copy(
            src_ref=src, dst_ref=dst, send_sem=send, recv_sem=recv,
            device_id=where, device_id_type=MESH,
        )

    loads = [
        pltpu.make_async_copy(src, dst, load_sem.at[n])
        for n, (src, dst) in enumerate(
            [
                (ei_hbm, ei), (si_hbm, si), (rl_hbm, rl), (og_hbm, og),
                (gp_hbm.at[0], gp), (up_hbm.at[0], up), (w_hbm.at[0], w),
            ]
        )
    ]
    for copy in loads:
        copy.start()

    barrier = pltpu.get_barrier_semaphore()
    peers = [device(xpeer(i), b, z, half) for i in range(1, nx)]
    peers += [device(x, bpeer(i), z, half) for i in range(1, nb)]
    peers += [device(x, bpeer(i), z, 1 - half) for i in range(nb)]
    peers += [device(x, b, zpeer(i), half) for i in range(1, nz)]
    for peer in peers:
        pl.semaphore_signal(barrier, inc=1, device_id=peer, device_id_type=MESH)

    for copy in loads[:4]:
        copy.wait()

    tokens = og.shape[1]
    share = jax.nn.sigmoid(rl[0:1, :] - rl[1:2, :])
    combine = [share.astype(BF16).astype(F32), (1.0 - share).astype(BF16).astype(F32)]
    chosen = []
    for k in range(2):
        ext[k, 0:head] = og[0:head]
        ext[k, LANES : 2 * LANES] = og[head:feats]
        ext[k, head:LANES] = jnp.where(
            iota((LANES - head, tokens), 0) == 0, combine[k], 0.0
        ).astype(BF16)
        slot = ei[k : k + 1] * cap + si[k : k + 1]
        chosen.append((iota((rows, tokens), 0) == slot).astype(F32).astype(BF16))

    xcopies = []
    for c in range(2):
        cols = slice(c * LANES, (c + 1) * LANES)
        outgoing = dot(chosen[0], ext[0, cols], ((1,), (1,)))
        outgoing += dot(chosen[1], ext[1, cols], ((1,), (1,)))
        xs[c] = outgoing.astype(BF16).reshape(nx, group, LANES)
        if c == 0:
            pl.semaphore_wait(barrier, len(peers))
        xcopies.append([
            remote(xs.at[c, xpeer(i)], xr.at[c, x], xsend.at[c, i], xrecv.at[c, x],
                   device(xpeer(i), b, z, half))
            for i in range(1, nx)
        ])
        for copy in xcopies[c]:
            copy.start()

    i_row = iota((rows, 1), 0)
    major = i_row // (nx * cap)
    rest = i_row - major * (nx * cap)
    minor = rest // cap
    source = minor * group + major * cap + (rest - minor * cap)
    perm[...] = (iota((rows, rows), 1) == source).astype(F32).astype(BF16)

    ycopies = [[None, None], [None, None]]
    for c in range(2):
        xr[c, x] = xs[c, x]
        with scope("x wait"):
            for i in range(1, nx):
                remote(xs.at[c, x], xr.at[c, xpeer(i)], xsend.at[c, i], xrecv.at[c, xpeer(i)],
                       device(xpeer(i), b, z, half)).wait_recv()
        turned = dot(perm[...], xr[c].reshape(rows, LANES)).astype(BF16)
        ys[c] = turned.reshape(nb, nx * cap, LANES)
        yr[0, c, b] = ys[c, b]
        ycopies[0][c] = [
            remote(ys.at[c, bpeer(i)], yr.at[0, c, b], ysend.at[0, c, i], yrecv.at[0, c, b],
                   device(x, bpeer(i), z, half))
            for i in range(1, nb)
        ]
        for copy in ycopies[0][c]:
            copy.start()
    for c in range(2):
        ycopies[1][c] = [
            remote(ys.at[c, bpeer(i)], yr.at[1, c, b], ysend.at[1, c, i], yrecv.at[1, c, b],
                   device(x, bpeer(i), z, 1 - half))
            for i in range(nb)
        ]
        for copy in ycopies[1][c]:
            copy.start()

    longer, shorter = nz // 2, nz - 1 - nz // 2
    hops = [(longer, shorter), (shorter, longer), (shorter, longer), (longer, shorter)]
    zcopies = []

    packs = LANES // (LANES - head)
    part = rows // packs

    def zref(q, src):
        return (g1 if q % 2 else g0).at[src, q // 2]

    def zsend_start(q, src, way):
        to = zpeer(1) if way == 0 else zpeer(-1)
        copy = remote(zref(q, src), zref(q, src), zsend.at[way, q, src], zrecv.at[q, src],
                      device(x, b, to, half))
        copy.start()
        zcopies.append(copy)

    def zwait(q, src):
        remote(zref(q, src), zref(q, src), zsend.at[0, q, src], zrecv.at[q, src],
               device(x, b, zpeer(1), half)).wait_recv()

    hid[...] = jnp.zeros_like(hid)
    unpacked[...] = jnp.zeros_like(unpacked)

    def work(q, src):
        h, c = q // 2, q % 2
        shard = src * 2 + (half if h == 0 else 1 - half)
        if c == 0:
            for n in range(packs):
                unpacked[n * part : (n + 1) * part, 0:head] = g0[
                    src, h, :, n * head : (n + 1) * head
                ]
        block = unpacked[...] if c == 0 else g1[src, h]
        cols = slice(c * LANES, (c + 1) * LANES)
        hid[...] += dot(wp[shard, :, cols], block, ((1,), (1,)))
        dgp[shard, :, cols] = dot(scaled_t[...], block).astype(BF16)

    for d in range(4 + nz // 2):
        ready = []
        if d < 4:
            h, c = d // 2, d % 2
            with scope("y wait"):
                for i in range(1 if h == 0 else 0, nb):
                    remote(ys.at[c, b], yr.at[h, c, bpeer(i)], ysend.at[h, c, i],
                           yrecv.at[h, c, bpeer(i)], device(x, bpeer(i), z, half)).wait_recv()
            canon = dot(perm[...], yr[h, c].reshape(rows, LANES),
                        ((0,), (0,)) if nx != nb else ((1,), (0,)))
            canon = canon.astype(BF16)
            if c == 0:
                for n in range(packs):
                    g0[z, h, :, n * head : (n + 1) * head] = canon[
                        n * part : (n + 1) * part, 0:head
                    ]
            else:
                g1[z, h] = canon
            zsend_start(d, z, 0)
            zsend_start(d, z, 1)
            ready.append((d, z))
        for q in range(4):
            s = d - q
            if s < 1:
                continue
            for way in range(2):
                if s <= hops[q][way]:
                    src = zpeer(-s) if way == 0 else zpeer(s)
                    with scope("z wait"):
                        zwait(q, src)
                    if s < hops[q][way]:
                        zsend_start(q, src, way)
                    ready.append((q, src))
        if d == 0:
            pick = (iota((8, LANES), 1) == head).astype(F32).astype(BF16)
            sw[...] = dot(pick, canon, ((1,), (1,)))[0:1]
            for copy in loads[4:]:
                copy.wait()
            for s in range(2 * nz):
                wp[s, :, 0:head] = w[:, s * feats : s * feats + head]
                wp[s, :, head:LANES] = jnp.zeros((hidden, LANES - head), BF16)
                wp[s, :, LANES : 2 * LANES] = w[:, s * feats + head : (s + 1) * feats]
            held = ready
            continue
        if d == 1:
            slot_weight = sw[...]
            gate = gp[...].astype(F32)
            upf = up[...].astype(F32)
            sigma = jax.nn.sigmoid(gate)
            silu = gate * sigma
            act[...] = silu * upf
            scaled_t[...] = (slot_weight * act[...]).astype(BF16)
            f1[...] = slot_weight * (upf * (sigma * (1.0 + gate * (1.0 - sigma))))
            f2[...] = slot_weight * silu
            i_row = iota((rows, 1), 0)
            i_x = i_row // group
            i_rest = i_row - i_x * group
            i_b = i_rest // cap
            i_lane = i_x * cap + (i_rest - i_b * cap)
            spread[...] = (iota((rows, LANES), 1) == i_lane).astype(F32)
            ready = held + ready
        with scope("matmuls"):
            for q, src in ready:
                work(q, src)

    probe = jnp.sum(hid[...] * act[...], axis=0, keepdims=True)
    j_row = iota((1, rows), 1)
    j_rest = j_row - (j_row // group) * group
    parted = jnp.where(iota((nb, rows), 0) == j_rest // cap, probe, 0.0)
    vz[z] = dot(parted, spread[...], precision=lax.Precision.HIGHEST)
    pz = [
        remote(vz.at[z], vz.at[z], pzsend.at[i], pzrecv.at[z], device(x, b, zpeer(i), half))
        for i in range(1, nz)
    ]
    for copy in pz:
        copy.start()

    gg[...] = (hid[...] * f1[...]).astype(BF16)
    ug[...] = (hid[...] * f2[...]).astype(BF16)
    stores = [
        pltpu.make_async_copy(gg, gg_hbm.at[0], store_sem.at[0]),
        pltpu.make_async_copy(ug, ug_hbm.at[0], store_sem.at[1]),
    ]
    for copy in stores:
        copy.start()

    with scope("sum z wait"):
        for i in range(1, nz):
            remote(vz.at[z], vz.at[zpeer(i)], pzsend.at[i], pzrecv.at[zpeer(i)],
                   device(x, b, zpeer(i), half)).wait_recv()
    vsum[...] = jnp.sum(vz[...], axis=0)
    vy[half, b] = vsum[...]
    py = [
        remote(vsum, vy.at[half, b], pysend.at[0, i], pyrecv.at[half, b],
               device(x, bpeer(i), z, half))
        for i in range(1, nb)
    ]
    py += [
        remote(vsum, vy.at[half, b], pysend.at[1, i], pyrecv.at[half, b],
               device(x, bpeer(i), z, 1 - half))
        for i in range(nb)
    ]
    for copy in py:
        copy.start()

    for s in range(2 * nz):
        dg[:, s * feats : s * feats + head] = dgp[s, :, 0:head]
        dg[:, s * feats + head : (s + 1) * feats] = dgp[s, :, LANES : 2 * LANES]
    stores.append(pltpu.make_async_copy(dg, dg_hbm.at[0], store_sem.at[2]))
    stores[-1].start()

    with scope("sum y wait"):
        for i in range(1, nb):
            remote(vsum, vy.at[half, bpeer(i)], pysend.at[0, i], pyrecv.at[half, bpeer(i)],
                   device(x, bpeer(i), z, half)).wait_recv()
        for i in range(nb):
            remote(vsum, vy.at[1 - half, bpeer(i)], pysend.at[1, i],
                   pyrecv.at[1 - half, bpeer(i)], device(x, bpeer(i), z, 1 - half)).wait_recv()
    mine = iota((nb, LANES), 0) == b
    for i in range(nb):
        both = vy[0, i] + vy[1, i]
        usum[i : i + 1, :] = jnp.sum(jnp.where(mine, both, 0.0), axis=0, keepdims=True)
    vx[x] = usum[...]
    px = [
        remote(usum, vx.at[x], pxsend.at[i], pxrecv.at[x], device(xpeer(i), b, z, half))
        for i in range(1, nx)
    ]
    for copy in px:
        copy.start()
    with scope("sum x wait"):
        for i in range(1, nx):
            remote(usum, vx.at[xpeer(i)], pxsend.at[i], pxrecv.at[xpeer(i)],
                   device(xpeer(i), b, z, half)).wait_recv()
    table = vx[...].reshape(nx * nb, LANES)
    token_probe = []
    for k in range(2):
        picked = (iota((nx * nb, tokens), 0) == ei[k : k + 1]).astype(F32)
        found = dot(table, picked, ((0,), (0,)), precision=lax.Precision.HIGHEST)
        lane = x * cap + si[k : k + 1]
        token_probe.append(
            jnp.sum(jnp.where(iota((LANES, tokens), 0) == lane, found, 0.0), axis=0, keepdims=True)
        )
    slope = (token_probe[0] - token_probe[1]) * share * (1.0 - share)
    rg[0:1] = slope
    rg[1:2] = -slope
    stores.append(pltpu.make_async_copy(rg, rg_hbm, store_sem.at[3]))
    stores[-1].start()

    with scope("end"):
        for c in range(2):
            for copy in xcopies[c]:
                copy.wait_send()
            for h in range(2):
                for copy in ycopies[h][c]:
                    copy.wait_send()
        for copy in zcopies + pz + py + px:
            copy.wait_send()
        for copy in stores:
            copy.wait()


def write_kernel(dg_in, gg_in, ug_in, rg_in, dg, gg, ug, rg, dg_v, gg_v, ug_v, rg_v, sem_in, sem_out):
    pieces = []
    for source, held, target in (
        (dg_in, dg_v, dg), (gg_in, gg_v, gg), (ug_in, ug_v, ug), (rg_in, rg_v, rg)
    ):
        height = source.shape[-2]
        step = 80 if source is dg_in else height
        for at in range(0, height, step):
            piece = pl.ds(at, min(step, height - at))
            if len(source.shape) == 3:
                pieces.append((source.at[0, piece], held.at[0, piece], target.at[0, piece]))
            else:
                pieces.append((source, held, target))
    reads = [
        pltpu.make_async_copy(source, held, sem_in.at[n])
        for n, (source, held, _) in enumerate(pieces)
    ]
    writes = [
        pltpu.make_async_copy(held, target, sem_out.at[n])
        for n, (_, held, target) in enumerate(pieces)
    ]
    for read in reads:
        read.start()
    for read, write in zip(reads, writes):
        read.wait()
        write.start()
    for write in writes:
        write.wait()


def shards(dims, out_grad, router_logits, expert_ids, slot_ids, down_weight, gate_pre, up_pre):
    nx, ny, nc, nz, cap = dims
    nb = ny * nc
    rows = nx * nb * cap
    tokens, feats = out_grad.shape
    hidden, width = down_weight.shape[1:]
    head = feats - LANES
    packs = LANES // (LANES - head)
    hbm = pl.BlockSpec(memory_space=pl.ANY)
    dma = pltpu.SemaphoreType.DMA
    results = pl.pallas_call(
        functools.partial(kernel, dims),
        out_shape=(
            jax.ShapeDtypeStruct(down_weight.shape, BF16),
            jax.ShapeDtypeStruct((1, hidden, rows), BF16),
            jax.ShapeDtypeStruct((1, hidden, rows), BF16),
            jax.ShapeDtypeStruct((2, tokens), F32),
        ),
        in_specs=[hbm] * 7,
        out_specs=(hbm,) * 4,
        scratch_shapes=[
            pltpu.VMEM((feats, tokens), BF16),
            pltpu.VMEM((2, tokens), F32),
            pltpu.VMEM((2, tokens), jnp.int32),
            pltpu.VMEM((2, tokens), jnp.int32),
            pltpu.VMEM((hidden, width), BF16),
            pltpu.VMEM((hidden, rows), BF16),
            pltpu.VMEM((hidden, rows), BF16),
            pltpu.VMEM((hidden, width), BF16),
            pltpu.VMEM((hidden, rows), BF16),
            pltpu.VMEM((hidden, rows), BF16),
            pltpu.VMEM((2, tokens), F32),
            pltpu.VMEM((rows, rows), BF16),
            pltpu.VMEM((rows, LANES), F32),
            pltpu.VMEM((2, 2 * LANES, tokens), BF16),
            pltpu.VMEM((2, nx, nb * cap, LANES), BF16),
            pltpu.VMEM((2, nx, nb * cap, LANES), BF16),
            pltpu.VMEM((2, nb, nx * cap, LANES), BF16),
            pltpu.VMEM((2, 2, nb, nx * cap, LANES), BF16),
            pltpu.VMEM((nz, 2, rows // packs, packs * head), BF16),
            pltpu.VMEM((nz, 2, rows, LANES), BF16),
            pltpu.VMEM((rows, LANES), BF16),
            pltpu.VMEM((1, rows), F32),
            pltpu.VMEM((2 * nz, hidden, 2 * LANES), BF16),
            pltpu.VMEM((2 * nz, hidden, 2 * LANES), BF16),
            pltpu.VMEM((hidden, rows), F32),
            pltpu.VMEM((hidden, rows), F32),
            pltpu.VMEM((hidden, rows), F32),
            pltpu.VMEM((hidden, rows), F32),
            pltpu.VMEM((hidden, rows), BF16),
            pltpu.VMEM((nz, nb, LANES), F32),
            pltpu.VMEM((2, nb, nb, LANES), F32),
            pltpu.VMEM((nx, nb, LANES), F32),
            pltpu.VMEM((nb, LANES), F32),
            pltpu.VMEM((nb, LANES), F32),
            dma((7,)),
            dma((4,)),
            dma((2, nx)),
            dma((2, nx)),
            dma((2, 2, nb)),
            dma((2, 2, nb)),
            dma((2, 4, nz)),
            dma((4, nz)),
            dma((nz,)),
            dma((nz,)),
            dma((2, nb)),
            dma((2, nb)),
            dma((nx,)),
            dma((nx,)),
        ],
        compiler_params=pltpu.CompilerParams(
            collective_id=0, has_side_effects=True, vmem_limit_bytes=VMEM_BYTES
        ),
    )(
        out_grad.T, router_logits.T, expert_ids.T, slot_ids.T, down_weight,
        gate_pre.transpose(0, 2, 1), up_pre.transpose(0, 2, 1),
    )
    down_grad, gate_grad, up_grad, router_grad = pl.pallas_call(
        write_kernel,
        out_shape=tuple(jax.ShapeDtypeStruct(r.shape, r.dtype) for r in results),
        in_specs=[hbm] * 4,
        out_specs=(hbm,) * 4,
        scratch_shapes=[pltpu.VMEM(r.shape, r.dtype) for r in results] + [dma((5,)), dma((5,))],
        compiler_params=pltpu.CompilerParams(vmem_limit_bytes=VMEM_BYTES),
    )(*results)
    return (
        down_grad, gate_grad.transpose(0, 2, 1), up_grad.transpose(0, 2, 1), router_grad.T
    )


def solution(mesh, dims=(8, 4, 2, 8, 12)):
    placed = (
        P("expert", "tensor"),
        P("expert", None),
        P("expert", None),
        P("expert", None),
        P("expert", "tensor", None),
        P("expert", None, "tensor"),
        P("expert", None, "tensor"),
    )
    return jax.shard_map(
        functools.partial(shards, dims),
        mesh=mesh,
        in_specs=placed,
        out_specs=(
            P("expert", "tensor", None),
            P("expert", None, "tensor"),
            P("expert", None, "tensor"),
            P("expert", None),
        ),
        check_vma=False,
    )
```

```python
import functools

import jax
import jax.numpy as jnp
from jax import lax
from jax.experimental import pallas as pl
from jax.experimental.pallas import tpu as pltpu
from jax.sharding import PartitionSpec as P

MESH = pl.DeviceIdType.MESH
BF16 = jnp.bfloat16
F32 = jnp.float32
LANES = 128
VMEM_BYTES = 62 * 1024 * 1024


def dot(a, b, contract=((1,), (0,))):
    return lax.dot_general(a, b, (contract, ((), ())), preferred_element_type=F32)


def thirds(v):
    first = v.astype(BF16)
    rest = v - first.astype(F32)
    second = rest.astype(BF16)
    return [first, second, (rest - second.astype(F32)).astype(BF16)]


def iota(shape, dim):
    return lax.broadcasted_iota(jnp.int32, shape, dim)


def kernel(
    dims, og_hbm, rl_hbm, ei_hbm, si_hbm, w_hbm, gp_hbm, up_hbm,
    dg_hbm, gg_hbm, ug_hbm, rg_hbm,
    og, rl, ei, si, w, gp, up, dg, gg, ug, rg,
    perm, order, spread, ext, xs, xr, ys, yr, g0, g1, unpacked, sw, wp, dgp, hid, act, f1, f2,
    scaled, vz, vy, vx, vsum, usum, load_sem, store_sem,
    xsend, xrecv, ysend, yrecv, zsend, zrecv, pzsend, pzrecv, pysend, pyrecv, pxsend, pxrecv,
):
    nx, ny, nc, nz, cap = dims
    nb = ny * nc
    rows = nx * nb * cap
    part_cap = cap // 2
    part_rows = rows // 2
    part_group = nb * part_cap
    feats, tokens = og.shape
    head = feats - LANES
    packs = LANES // (LANES - head)
    packed_rows = part_rows // packs
    hidden = w.shape[0]
    e, t = lax.axis_index("expert"), lax.axis_index("tensor")
    x, b = e // nb, e % nb
    z, half = t // 2, t % 2

    def xpeer(i):
        return lax.rem(x + i, nx)

    def bpeer(i):
        return lax.rem(b + i, nb)

    def zpeer(i):
        return lax.rem(z + i + nz, nz)

    def device(x_, b_, z_, half_):
        return {"expert": x_ * nb + b_, "tensor": z_ * 2 + half_}

    def farthest(n):
        return sorted(range(1, n), key=lambda i: -min(i, n - i))

    def remote(src, dst, send, recv, where):
        return pltpu.make_async_remote_copy(
            src_ref=src, dst_ref=dst, send_sem=send, recv_sem=recv,
            device_id=where, device_id_type=MESH,
        )

    loads = [
        pltpu.make_async_copy(src, dst, load_sem.at[n])
        for n, (src, dst) in enumerate(
            [
                (ei_hbm, ei), (si_hbm, si), (rl_hbm, rl), (og_hbm, og),
                (gp_hbm.at[0], gp), (up_hbm.at[0], up), (w_hbm.at[0], w),
            ]
        )
    ]
    for copy in loads:
        copy.start()

    barrier = pltpu.get_barrier_semaphore()
    peers = [device(xpeer(i), b, z, half) for i in farthest(nx)]
    peers += [device(x, bpeer(i), z, half) for i in range(1, nb)]
    peers += [device(x, bpeer(i), z, 1 - half) for i in range(nb)]
    peers += [device(x, b, zpeer(i), half) for i in range(1, nz)]
    for peer in peers:
        pl.semaphore_signal(barrier, inc=1, device_id=peer, device_id_type=MESH)

    for copy in loads[:4]:
        copy.wait()

    share = jax.nn.sigmoid(rl[0:1, :] - rl[1:2, :])
    combine = [share.astype(BF16).astype(F32), (1.0 - share).astype(BF16).astype(F32)]
    chosen = [[], []]
    for k in range(2):
        ext[k, 0:head] = og[0:head]
        ext[k, LANES : 2 * LANES] = og[head:feats]
        ext[k, head:LANES] = jnp.where(
            iota((LANES - head, tokens), 0) == 0, combine[k], 0.0
        ).astype(BF16)
        for r in range(2):
            place = si[k : k + 1] - r * part_cap
            inside = (place >= 0) & (place < part_cap)
            row = jnp.where(inside, ei[k : k + 1] * part_cap + place, -1)
            chosen[r].append((iota((part_rows, tokens), 0) == row).astype(F32).astype(BF16))

    chunks = [(c, r) for c in range(2) for r in range(2)]
    xcopies = []
    for c, r in chunks:
        cols = slice(c * LANES, (c + 1) * LANES)
        outgoing = dot(chosen[r][0], ext[0, cols], ((1,), (1,)))
        outgoing += dot(chosen[r][1], ext[1, cols], ((1,), (1,)))
        xs[c, r] = outgoing.astype(BF16).reshape(nx, part_group, LANES)
        if (c, r) == (0, 0):
            pl.semaphore_wait(barrier, len(peers))
        for i in farthest(nx):
            copy = remote(xs.at[c, r, xpeer(i)], xr.at[c, r, x], xsend.at[c, r, i],
                          xrecv.at[c, r, x], device(xpeer(i), b, z, half))
            copy.start()
            xcopies.append(copy)

    i_row = iota((part_rows, 1), 0)
    major = i_row // (nx * part_cap)
    rest = i_row - major * (nx * part_cap)
    minor = rest // part_cap
    source = minor * part_group + major * part_cap + (rest - minor * part_cap)
    perm[...] = (iota((part_rows, part_rows), 1) == source).astype(F32).astype(BF16)

    n_lane = iota((1, rows), 1)
    n_part = n_lane // part_rows
    n_rest = n_lane - n_part * part_rows
    n_source = n_rest // part_cap
    n_slot = n_rest - n_source * part_cap
    origin = n_source * cap + n_part * part_cap + n_slot
    order[...] = (iota((rows, rows), 0) == origin).astype(F32).astype(BF16)

    i_row = iota((rows, 1), 0)
    i_part = i_row // part_rows
    i_rest = i_row - i_part * part_rows
    i_source = i_rest // part_cap
    i_lane = (i_source // nb) * cap + i_part * part_cap + (i_rest - i_source * part_cap)
    spread[...] = (iota((rows, LANES), 1) == i_lane).astype(F32).astype(BF16)

    for copy in loads[4:]:
        copy.wait()
    for s in range(2 * nz):
        wp[s, :, 0:head] = w[:, s * feats : s * feats + head]
        wp[s, :, head:LANES] = jnp.zeros((hidden, LANES - head), BF16)
        wp[s, :, LANES : 2 * LANES] = w[:, s * feats + head : (s + 1) * feats]
    gate = dot(gp[...], order[...])
    upf = dot(up[...], order[...])
    sigma = jax.nn.sigmoid(gate)
    silu = gate * sigma
    act[...] = silu * upf
    f1[...] = upf * (sigma * (1.0 + gate * (1.0 - sigma)))
    f2[...] = silu
    hid[...] = jnp.zeros_like(hid)
    unpacked[...] = jnp.zeros_like(unpacked)

    ycopies = []

    def ysend_start(c, r, h):
        for i in range(1 - h, nb):
            copy = remote(ys.at[c, r, bpeer(i)], yr.at[h, c, r, b], ysend.at[h, c, r, i],
                          yrecv.at[h, c, r, b],
                          device(x, bpeer(i), z, half if h == 0 else 1 - half))
            copy.start()
            ycopies.append(copy)

    for c, r in chunks:
        xr[c, r, x] = xs[c, r, x]
        for i in range(1, nx):
            remote(xs.at[c, r, x], xr.at[c, r, xpeer(i)], xsend.at[c, r, i],
                   xrecv.at[c, r, xpeer(i)], device(xpeer(i), b, z, half)).wait_recv()
        turned = dot(perm[...], xr[c, r].reshape(part_rows, LANES)).astype(BF16)
        ys[c, r] = turned.reshape(nb, nx * part_cap, LANES)
        yr[0, c, r, b] = ys[c, r, b]
        ysend_start(c, r, 0)

    longer, shorter = nz // 2, nz - 1 - nz // 2
    hops = [(longer, shorter), (shorter, longer), (shorter, longer), (longer, shorter)]
    zcopies = []

    def zref(q, src):
        h, c, r = q // 4, q // 2 % 2, q % 2
        return (g1 if c else g0).at[src, h, r]

    def zsend_start(q, src, way):
        to = zpeer(1) if way == 0 else zpeer(-1)
        copy = remote(zref(q, src), zref(q, src), zsend.at[way, q, src], zrecv.at[q, src],
                      device(x, b, to, half))
        copy.start()
        zcopies.append(copy)

    def zwait(q, src):
        remote(zref(q, src), zref(q, src), zsend.at[0, q, src], zrecv.at[q, src],
               device(x, b, zpeer(1), half)).wait_recv()

    def hidden_part(q, src):
        h, c = q // 4, q // 2 % 2
        shard = src * 2 + (half if h == 0 else 1 - half)
        if c == 0:
            for r in range(2):
                for n in range(packs):
                    at = r * part_rows + n * packed_rows
                    unpacked[at : at + packed_rows, 0:head] = g0[
                        src, h, r, :, n * head : (n + 1) * head
                    ]
            block = unpacked[...]
        else:
            block = g1[src, h].reshape(rows, LANES)
        hid[...] += dot(wp[shard, :, c * LANES : (c + 1) * LANES], block, ((1,), (1,)))
        return block, shard, slice(c * LANES, (c + 1) * LANES)

    def down_part(block, shard, cols):
        dgp[shard, :, cols] = dot(scaled[...], block).astype(BF16)

    def own(q):
        h, c, r = q // 4, q // 2 % 2, q % 2
        for i in range(1 - h, nb):
            remote(ys.at[c, r, b], yr.at[h, c, r, bpeer(i)], ysend.at[h, c, r, i],
                   yrecv.at[h, c, r, bpeer(i)], device(x, bpeer(i), z, half)).wait_recv()
        canon = dot(perm[...], yr[h, c, r].reshape(part_rows, LANES),
                    ((0,), (0,)) if nx != nb else ((1,), (0,))).astype(BF16)
        if c == 0:
            for n in range(packs):
                g0[z, h, r, :, n * head : (n + 1) * head] = canon[
                    n * packed_rows : (n + 1) * packed_rows, 0:head
                ]
        else:
            g1[z, h, r] = canon
        zsend_start(q, z, 0)
        zsend_start(q, z, 1)
        if q < 2:
            pick = (iota((8, LANES), 1) == head).astype(F32).astype(BF16)
            sw[:, q * part_rows : (q + 1) * part_rows] = dot(pick, canon, ((1,), (1,)))[0:1]

    steps = [(0, s) for s in range(nz // 2)] + [(1, 0), (0, nz // 2)]
    steps += [(1, s) for s in range(1, nz // 2 + 1)]
    later = []
    for n, (h, s) in enumerate(steps):
        done = []
        if s == 0:
            for q in range(4 * h, 4 * h + 4):
                own(q)
                if q % 2 == 1:
                    done.append((q, z))
            if h == 0:
                scaled[...] = (sw[...] * act[...]).astype(BF16)
                for c, r in chunks:
                    ysend_start(c, r, 1)
        else:
            for turn in range(2):
                for r in range(2):
                    for way in range(2):
                        c = turn if hops[2 * h][way] > hops[2 * h + 1][way] else 1 - turn
                        q = 4 * h + 2 * c + r
                        if s <= hops[2 * h + c][way]:
                            src = zpeer(-s) if way == 0 else zpeer(s)
                            zwait(q, src)
                            if s < hops[2 * h + c][way]:
                                zsend_start(q, src, way)
                            if r == 1:
                                done.append((q, src))
        for q, src in done:
            rest = hidden_part(q, src)
            if n < len(steps) - 1:
                down_part(*rest)
            else:
                later.append(rest)

    probe = jnp.sum(hid[...] * act[...], axis=0, keepdims=True)
    parted = jnp.where(iota((nb, rows), 0) == n_source - (n_source // nb) * nb, probe, 0.0)
    parts = dot(jnp.concatenate(thirds(parted), axis=0), spread[...])
    vz[z] = parts[0:nb] + parts[nb : 2 * nb] + parts[2 * nb : 3 * nb]
    pz = [
        remote(vz.at[z], vz.at[z], pzsend.at[i], pzrecv.at[z], device(x, b, zpeer(i), half))
        for i in farthest(nz)
    ]
    for copy in pz:
        copy.start()

    for rest in later:
        down_part(*rest)
    gg[...] = dot((hid[...] * (sw[...] * f1[...])).astype(BF16), order[...], ((1,), (1,))).astype(BF16)
    ug[...] = dot((hid[...] * (sw[...] * f2[...])).astype(BF16), order[...], ((1,), (1,))).astype(BF16)
    stores = [
        pltpu.make_async_copy(gg, gg_hbm.at[0], store_sem.at[0]),
        pltpu.make_async_copy(ug, ug_hbm.at[0], store_sem.at[1]),
    ]
    for copy in stores:
        copy.start()

    for i in range(1, nz):
        remote(vz.at[z], vz.at[zpeer(i)], pzsend.at[i], pzrecv.at[zpeer(i)],
               device(x, b, zpeer(i), half)).wait_recv()
    vsum[...] = jnp.sum(vz[...], axis=0)
    vy[half, b] = vsum[...]
    py = [
        remote(vsum, vy.at[half, b], pysend.at[1, i], pyrecv.at[half, b],
               device(x, bpeer(i), z, 1 - half))
        for i in range(nb)
    ]
    py += [
        remote(vsum, vy.at[half, b], pysend.at[0, i], pyrecv.at[half, b],
               device(x, bpeer(i), z, half))
        for i in range(1, nb)
    ]
    for copy in py:
        copy.start()

    for s in range(2 * nz):
        dg[:, s * feats : s * feats + head] = dgp[s, :, 0:head]
        dg[:, s * feats + head : (s + 1) * feats] = dgp[s, :, LANES : 2 * LANES]
    stores.append(pltpu.make_async_copy(dg, dg_hbm.at[0], store_sem.at[2]))
    stores[-1].start()

    for i in range(1, nb):
        remote(vsum, vy.at[half, bpeer(i)], pysend.at[0, i], pyrecv.at[half, bpeer(i)],
               device(x, bpeer(i), z, half)).wait_recv()
    for i in range(nb):
        remote(vsum, vy.at[1 - half, bpeer(i)], pysend.at[1, i],
               pyrecv.at[1 - half, bpeer(i)], device(x, bpeer(i), z, 1 - half)).wait_recv()
    mine = iota((nb, LANES), 0) == b
    for i in range(nb):
        both = vy[0, i] + vy[1, i]
        usum[i : i + 1, :] = jnp.sum(jnp.where(mine, both, 0.0), axis=0, keepdims=True)
    vx[x] = usum[...]
    px = [
        remote(usum, vx.at[x], pxsend.at[i], pxrecv.at[x], device(xpeer(i), b, z, half))
        for i in farthest(nx)
    ]
    for copy in px:
        copy.start()
    for i in range(1, nx):
        remote(usum, vx.at[xpeer(i)], pxsend.at[i], pxrecv.at[xpeer(i)],
               device(xpeer(i), b, z, half)).wait_recv()
    table = jnp.concatenate(thirds(vx[...].reshape(nx * nb, LANES)), axis=0)
    token_probe = []
    for k in range(2):
        picked = (iota((nx * nb, tokens), 0) == ei[k : k + 1]).astype(F32).astype(BF16)
        found = dot(table, jnp.concatenate([picked] * 3, axis=0), ((0,), (0,)))
        lane = x * cap + si[k : k + 1]
        token_probe.append(
            jnp.sum(jnp.where(iota((LANES, tokens), 0) == lane, found, 0.0), axis=0, keepdims=True)
        )
    slope = (token_probe[0] - token_probe[1]) * share * (1.0 - share)
    rg[0:1] = slope
    rg[1:2] = -slope
    stores.append(pltpu.make_async_copy(rg, rg_hbm, store_sem.at[3]))
    stores[-1].start()

    for copy in xcopies + ycopies + zcopies + pz + py + px:
        copy.wait_send()
    for copy in stores:
        copy.wait()


def write_kernel(dg_in, gg_in, ug_in, rg_in, dg, gg, ug, rg, dg_v, gg_v, ug_v, rg_v, sem_in, sem_out):
    pieces = []
    for source, held, target in (
        (dg_in, dg_v, dg), (gg_in, gg_v, gg), (ug_in, ug_v, ug), (rg_in, rg_v, rg)
    ):
        height = source.shape[-2]
        step = 80 if source is dg_in else height
        for at in range(0, height, step):
            piece = pl.ds(at, min(step, height - at))
            if len(source.shape) == 3:
                pieces.append((source.at[0, piece], held.at[0, piece], target.at[0, piece]))
            else:
                pieces.append((source, held, target))
    reads = [
        pltpu.make_async_copy(source, held, sem_in.at[n])
        for n, (source, held, _) in enumerate(pieces)
    ]
    writes = [
        pltpu.make_async_copy(held, target, sem_out.at[n])
        for n, (_, held, target) in enumerate(pieces)
    ]
    for read in reads:
        read.start()
    for read, write in zip(reads, writes):
        read.wait()
        write.start()
    for write in writes:
        write.wait()


def shards(dims, out_grad, router_logits, expert_ids, slot_ids, down_weight, gate_pre, up_pre):
    nx, ny, nc, nz, cap = dims
    nb = ny * nc
    rows = nx * nb * cap
    tokens, feats = out_grad.shape
    hidden, width = down_weight.shape[1:]
    head = feats - LANES
    packs = LANES // (LANES - head)
    hbm = pl.BlockSpec(memory_space=pl.ANY)
    dma = pltpu.SemaphoreType.DMA
    results = pl.pallas_call(
        functools.partial(kernel, dims),
        out_shape=(
            jax.ShapeDtypeStruct(down_weight.shape, BF16),
            jax.ShapeDtypeStruct((1, hidden, rows), BF16),
            jax.ShapeDtypeStruct((1, hidden, rows), BF16),
            jax.ShapeDtypeStruct((2, tokens), F32),
        ),
        in_specs=[hbm] * 7,
        out_specs=(hbm,) * 4,
        scratch_shapes=[
            pltpu.VMEM((feats, tokens), BF16),
            pltpu.VMEM((2, tokens), F32),
            pltpu.VMEM((2, tokens), jnp.int32),
            pltpu.VMEM((2, tokens), jnp.int32),
            pltpu.VMEM((hidden, width), BF16),
            pltpu.VMEM((hidden, rows), BF16),
            pltpu.VMEM((hidden, rows), BF16),
            pltpu.VMEM((hidden, width), BF16),
            pltpu.VMEM((hidden, rows), BF16),
            pltpu.VMEM((hidden, rows), BF16),
            pltpu.VMEM((2, tokens), F32),
            pltpu.VMEM((rows // 2, rows // 2), BF16),
            pltpu.VMEM((rows, rows), BF16),
            pltpu.VMEM((rows, LANES), BF16),
            pltpu.VMEM((2, 2 * LANES, tokens), BF16),
            pltpu.VMEM((2, 2, nx, nb * cap // 2, LANES), BF16),
            pltpu.VMEM((2, 2, nx, nb * cap // 2, LANES), BF16),
            pltpu.VMEM((2, 2, nb, nx * cap // 2, LANES), BF16),
            pltpu.VMEM((2, 2, 2, nb, nx * cap // 2, LANES), BF16),
            pltpu.VMEM((nz, 2, 2, rows // 2 // packs, packs * head), BF16),
            pltpu.VMEM((nz, 2, 2, rows // 2, LANES), BF16),
            pltpu.VMEM((rows, LANES), BF16),
            pltpu.VMEM((1, rows), F32),
            pltpu.VMEM((2 * nz, hidden, 2 * LANES), BF16),
            pltpu.VMEM((2 * nz, hidden, 2 * LANES), BF16),
            pltpu.VMEM((hidden, rows), F32),
            pltpu.VMEM((hidden, rows), F32),
            pltpu.VMEM((hidden, rows), F32),
            pltpu.VMEM((hidden, rows), F32),
            pltpu.VMEM((hidden, rows), BF16),
            pltpu.VMEM((nz, nb, LANES), F32),
            pltpu.VMEM((2, nb, nb, LANES), F32),
            pltpu.VMEM((nx, nb, LANES), F32),
            pltpu.VMEM((nb, LANES), F32),
            pltpu.VMEM((nb, LANES), F32),
            dma((7,)),
            dma((4,)),
            dma((2, 2, nx)),
            dma((2, 2, nx)),
            dma((2, 2, 2, nb)),
            dma((2, 2, 2, nb)),
            dma((2, 8, nz)),
            dma((8, nz)),
            dma((nz,)),
            dma((nz,)),
            dma((2, nb)),
            dma((2, nb)),
            dma((nx,)),
            dma((nx,)),
        ],
        compiler_params=pltpu.CompilerParams(
            collective_id=0, has_side_effects=True, vmem_limit_bytes=VMEM_BYTES
        ),
    )(
        out_grad.T, router_logits.T, expert_ids.T, slot_ids.T, down_weight,
        gate_pre.transpose(0, 2, 1), up_pre.transpose(0, 2, 1),
    )
    down_grad, gate_grad, up_grad, router_grad = pl.pallas_call(
        write_kernel,
        out_shape=tuple(jax.ShapeDtypeStruct(r.shape, r.dtype) for r in results),
        in_specs=[hbm] * 4,
        out_specs=(hbm,) * 4,
        scratch_shapes=[pltpu.VMEM(r.shape, r.dtype) for r in results] + [dma((5,)), dma((5,))],
        compiler_params=pltpu.CompilerParams(vmem_limit_bytes=VMEM_BYTES),
    )(*results)
    return (
        down_grad, gate_grad.transpose(0, 2, 1), up_grad.transpose(0, 2, 1), router_grad.T
    )


def solution(mesh, dims=(8, 4, 2, 8, 12)):
    placed = (
        P("expert", "tensor"),
        P("expert", None),
        P("expert", None),
        P("expert", None),
        P("expert", "tensor", None),
        P("expert", None, "tensor"),
        P("expert", None, "tensor"),
    )
    return jax.shard_map(
        functools.partial(shards, dims),
        mesh=mesh,
        in_specs=placed,
        out_specs=(
            P("expert", "tensor", None),
            P("expert", None, "tensor"),
            P("expert", None, "tensor"),
            P("expert", None),
        ),
        check_vma=False,
    )
```

```python
import functools

import jax
import jax.numpy as jnp
from jax import lax
from jax.experimental import pallas as pl
from jax.experimental.pallas import tpu as pltpu
from jax.sharding import PartitionSpec as P

MESH = pl.DeviceIdType.MESH
BF16 = jnp.bfloat16
F32 = jnp.float32
LANES = 128
VMEM_BYTES = 62 * 1024 * 1024


def dot(a, b, contract=((1,), (0,))):
    return lax.dot_general(a, b, (contract, ((), ())), preferred_element_type=F32)


def thirds(v):
    first = v.astype(BF16)
    rest = v - first.astype(F32)
    second = rest.astype(BF16)
    return [first, second, (rest - second.astype(F32)).astype(BF16)]


def iota(shape, dim):
    return lax.broadcasted_iota(jnp.int32, shape, dim)


def kernel(
    dims, og_hbm, rl_hbm, ei_hbm, si_hbm, w_hbm, gp_hbm, up_hbm,
    dg_hbm, gg_hbm, ug_hbm, rg_hbm,
    og, rl, ei, si, w, gp, up, dg, gg, ug, rg,
    perm, order, spread, ext, xs, xr, ys, yr, g0, g1, unpacked, sw, wp, dgp, hid, act, f1, f2,
    scaled, vz, vy, vx, vsum, usum, load_sem, store_sem,
    xsend, xrecv, ysend, yrecv, zsend, zrecv, asend, arecv, pzsend, pzrecv, pysend, pyrecv, pxsend, pxrecv,
):
    nx, ny, nc, nz, cap = dims
    nb = ny * nc
    rows = nx * nb * cap
    part_cap = cap // 2
    part_rows = rows // 2
    part_group = nb * part_cap
    feats, tokens = og.shape
    head = feats - LANES
    packs = LANES // (LANES - head)
    packed_rows = part_rows // packs
    hidden = w.shape[0]
    e, t = lax.axis_index("expert"), lax.axis_index("tensor")
    x, b = e // nb, e % nb
    z, half = t // 2, t % 2

    def xpeer(i):
        return lax.rem(x + i, nx)

    def bpeer(i):
        return lax.rem(b + i, nb)

    def zpeer(i):
        return lax.rem(z + i + nz, nz)

    def device(x_, b_, z_, half_):
        return {"expert": x_ * nb + b_, "tensor": z_ * 2 + half_}

    def farthest(n):
        return sorted(range(1, n), key=lambda i: -min(i, n - i))

    def remote(src, dst, send, recv, where):
        return pltpu.make_async_remote_copy(
            src_ref=src, dst_ref=dst, send_sem=send, recv_sem=recv,
            device_id=where, device_id_type=MESH,
        )

    loads = [
        pltpu.make_async_copy(src, dst, load_sem.at[n])
        for n, (src, dst) in enumerate(
            [
                (ei_hbm, ei), (si_hbm, si), (rl_hbm, rl), (og_hbm, og),
                (gp_hbm.at[0], gp), (up_hbm.at[0], up), (w_hbm.at[0], w),
            ]
        )
    ]
    for copy in loads:
        copy.start()

    barrier = pltpu.get_barrier_semaphore()
    peers = [device(xpeer(i), b, z, half) for i in farthest(nx)]
    peers += [device(x, bpeer(i), z, half) for i in range(1, nb)]
    peers += [device(x, bpeer(i), z, 1 - half) for i in range(nb)]
    peers += [device(x, b, zpeer(i), half) for i in range(1, nz)]
    for peer in peers:
        pl.semaphore_signal(barrier, inc=1, device_id=peer, device_id_type=MESH)

    for copy in loads[:4]:
        copy.wait()

    share = jax.nn.sigmoid(rl[0:1, :] - rl[1:2, :])
    combine = [share.astype(BF16).astype(F32), (1.0 - share).astype(BF16).astype(F32)]
    chosen = [[], []]
    for k in range(2):
        ext[k, 0:head] = og[0:head]
        ext[k, LANES : 2 * LANES] = og[head:feats]
        ext[k, head:LANES] = jnp.where(
            iota((LANES - head, tokens), 0) == 0, combine[k], 0.0
        ).astype(BF16)
        for r in range(2):
            place = si[k : k + 1] - r * part_cap
            inside = (place >= 0) & (place < part_cap)
            row = jnp.where(inside, ei[k : k + 1] * part_cap + place, -1)
            chosen[r].append((iota((part_rows, tokens), 0) == row).astype(F32).astype(BF16))

    chunks = [(c, r) for c in range(2) for r in range(2)]
    xcopies = []
    for c, r in chunks:
        cols = slice(c * LANES, (c + 1) * LANES)
        outgoing = dot(chosen[r][0], ext[0, cols], ((1,), (1,)))
        outgoing += dot(chosen[r][1], ext[1, cols], ((1,), (1,)))
        xs[c, r] = outgoing.astype(BF16).reshape(nx, part_group, LANES)
        if (c, r) == (0, 0):
            pl.semaphore_wait(barrier, len(peers))
        for i in farthest(nx):
            copy = remote(xs.at[c, r, xpeer(i)], xr.at[c, r, x], xsend.at[c, r, i],
                          xrecv.at[c, r, x], device(xpeer(i), b, z, half))
            copy.start()
            xcopies.append(copy)

    i_row = iota((part_rows, 1), 0)
    major = i_row // (nx * part_cap)
    rest = i_row - major * (nx * part_cap)
    minor = rest // part_cap
    source = minor * part_group + major * part_cap + (rest - minor * part_cap)
    perm[...] = (iota((part_rows, part_rows), 1) == source).astype(F32).astype(BF16)

    n_lane = iota((1, rows), 1)
    n_part = n_lane // part_rows
    n_rest = n_lane - n_part * part_rows
    n_source = n_rest // part_cap
    n_slot = n_rest - n_source * part_cap
    origin = n_source * cap + n_part * part_cap + n_slot
    order[...] = (iota((rows, rows), 0) == origin).astype(F32).astype(BF16)

    i_row = iota((rows, 1), 0)
    i_part = i_row // part_rows
    i_rest = i_row - i_part * part_rows
    i_source = i_rest // part_cap
    i_lane = (i_source // nb) * cap + i_part * part_cap + (i_rest - i_source * part_cap)
    spread[...] = (iota((rows, LANES), 1) == i_lane).astype(F32).astype(BF16)

    for copy in loads[4:]:
        copy.wait()
    for s in range(2 * nz):
        wp[s, :, 0:head] = w[:, s * feats : s * feats + head]
        wp[s, :, head:LANES] = jnp.zeros((hidden, LANES - head), BF16)
        wp[s, :, LANES : 2 * LANES] = w[:, s * feats + head : (s + 1) * feats]
    gate = dot(gp[...], order[...])
    upf = dot(up[...], order[...])
    sigma = jax.nn.sigmoid(gate)
    silu = gate * sigma
    act[...] = silu * upf
    f1[...] = upf * (sigma * (1.0 + gate * (1.0 - sigma)))
    f2[...] = silu
    hid[...] = jnp.zeros_like(hid)
    unpacked[...] = jnp.zeros_like(unpacked)

    ycopies = []

    def ysend_start(c, r, h):
        for i in range(1 - h, nb):
            copy = remote(ys.at[c, r, bpeer(i)], yr.at[h, c, r, b], ysend.at[h, c, r, i],
                          yrecv.at[h, c, r, b],
                          device(x, bpeer(i), z, half if h == 0 else 1 - half))
            copy.start()
            ycopies.append(copy)

    for c, r in chunks:
        xr[c, r, x] = xs[c, r, x]
        for i in range(1, nx):
            remote(xs.at[c, r, x], xr.at[c, r, xpeer(i)], xsend.at[c, r, i],
                   xrecv.at[c, r, xpeer(i)], device(xpeer(i), b, z, half)).wait_recv()
        turned = dot(perm[...], xr[c, r].reshape(part_rows, LANES)).astype(BF16)
        ys[c, r] = turned.reshape(nb, nx * part_cap, LANES)
        yr[0, c, r, b] = ys[c, r, b]
        ysend_start(c, r, 0)

    longer, shorter = nz // 2, nz - 1 - nz // 2
    hops = [(longer, shorter), (shorter, longer), (shorter, shorter), (shorter, shorter)]
    zcopies = []

    def zref(q, src):
        h, c, r = q // 4, q // 2 % 2, q % 2
        return (g1 if c else g0).at[src, h, r]

    def zsend_start(q, src, way):
        to = zpeer(1) if way == 0 else zpeer(-1)
        copy = remote(zref(q, src), zref(q, src), zsend.at[way, q, src], zrecv.at[q, src],
                      device(x, b, to, half))
        copy.start()
        zcopies.append(copy)

    def zwait(q, src):
        remote(zref(q, src), zref(q, src), zsend.at[0, q, src], zrecv.at[q, src],
               device(x, b, zpeer(1), half)).wait_recv()

    def across(q, src):
        return remote(zref(q, src), zref(q + 4, src), asend.at[q], arecv.at[q],
                      device(x, b, z, 1 - half))

    def block_of(q, src):
        h, c = q // 4, q // 2 % 2
        if c == 1:
            return g1[src, h].reshape(rows, LANES)
        for r in range(2):
            for n in range(packs):
                at = r * part_rows + n * packed_rows
                unpacked[at : at + packed_rows, 0:head] = g0[
                    src, h, r, :, n * head : (n + 1) * head
                ]
        return unpacked[...]

    def place_of(q, src):
        h, c = q // 4, q // 2 % 2
        return src * 2 + (half if h == 0 else 1 - half), slice(c * LANES, (c + 1) * LANES)

    def hidden_part(q, src, block):
        shard, cols = place_of(q, src)
        hid[...] += dot(wp[shard, :, cols], block, ((1,), (1,)))

    def down_part(q, src, block):
        shard, cols = place_of(q, src)
        dgp[shard, :, cols] = dot(scaled[...], block).astype(BF16)

    def own(q):
        h, c, r = q // 4, q // 2 % 2, q % 2
        for i in range(1 - h, nb):
            remote(ys.at[c, r, b], yr.at[h, c, r, bpeer(i)], ysend.at[h, c, r, i],
                   yrecv.at[h, c, r, bpeer(i)], device(x, bpeer(i), z, half)).wait_recv()
        canon = dot(perm[...], yr[h, c, r].reshape(part_rows, LANES),
                    ((0,), (0,)) if nx != nb else ((1,), (0,))).astype(BF16)
        if c == 0:
            for n in range(packs):
                g0[z, h, r, :, n * head : (n + 1) * head] = canon[
                    n * packed_rows : (n + 1) * packed_rows, 0:head
                ]
        else:
            g1[z, h, r] = canon
        zsend_start(q, z, 0)
        zsend_start(q, z, 1)
        if q < 2:
            pick = (iota((8, LANES), 1) == head).astype(F32).astype(BF16)
            sw[:, q * part_rows : (q + 1) * part_rows] = dot(pick, canon, ((1,), (1,)))[0:1]

    steps = [(0, s) for s in range(nz // 2)] + [(1, 0), (0, nz // 2)]
    steps += [(1, s) for s in range(1, nz // 2 + 1)]
    later = []
    for n, (h, s) in enumerate(steps):
        done = []
        if s == 0:
            for q in range(4 * h, 4 * h + 4):
                own(q)
                if q % 2 == 1:
                    done.append((q, z))
            if h == 0:
                scaled[...] = (sw[...] * act[...]).astype(BF16)
                for c, r in chunks:
                    ysend_start(c, r, 1)
        else:
            for turn in range(2):
                for r in range(2):
                    for way in range(2):
                        c = turn if hops[2 * h][way] >= hops[2 * h + 1][way] else 1 - turn
                        q = 4 * h + 2 * c + r
                        if s <= hops[2 * h + c][way]:
                            src = zpeer(-s) if way == 0 else zpeer(s)
                            zwait(q, src)
                            if s < hops[2 * h + c][way]:
                                zsend_start(q, src, way)
                            if h == 0 and s == longer:
                                copy = across(q, src)
                                copy.start()
                                zcopies.append(copy)
                            if r == 1:
                                done.append((q, src))
            if h == 1 and s == longer:
                for q in range(4):
                    across(q, zpeer(longer)).wait_recv()
                done += [(5, zpeer(longer)), (7, zpeer(longer))]
        for q, src in done:
            block = block_of(q, src)
            hidden_part(q, src, block)
            if n < len(steps) - 2:
                down_part(q, src, block)
            else:
                later.append((q, src))

    probe = jnp.sum(hid[...] * act[...], axis=0, keepdims=True)
    parted = jnp.where(iota((nb, rows), 0) == n_source - (n_source // nb) * nb, probe, 0.0)
    parts = dot(jnp.concatenate(thirds(parted), axis=0), spread[...])
    vz[z] = parts[0:nb] + parts[nb : 2 * nb] + parts[2 * nb : 3 * nb]
    pz = [
        remote(vz.at[z], vz.at[z], pzsend.at[i], pzrecv.at[z], device(x, b, zpeer(i), half))
        for i in farthest(nz)
    ]
    for copy in pz:
        copy.start()

    gg[...] = dot((hid[...] * (sw[...] * f1[...])).astype(BF16), order[...], ((1,), (1,))).astype(BF16)
    ug[...] = dot((hid[...] * (sw[...] * f2[...])).astype(BF16), order[...], ((1,), (1,))).astype(BF16)
    stores = [
        pltpu.make_async_copy(gg, gg_hbm.at[0], store_sem.at[0]),
        pltpu.make_async_copy(ug, ug_hbm.at[0], store_sem.at[1]),
    ]
    for copy in stores:
        copy.start()

    for i in range(1, nz):
        remote(vz.at[z], vz.at[zpeer(i)], pzsend.at[i], pzrecv.at[zpeer(i)],
               device(x, b, zpeer(i), half)).wait_recv()
    vsum[...] = jnp.sum(vz[...], axis=0)
    vy[half, b] = vsum[...]
    py = [
        remote(vsum, vy.at[half, b], pysend.at[1, i], pyrecv.at[half, b],
               device(x, bpeer(i), z, 1 - half))
        for i in range(nb)
    ]
    py += [
        remote(vsum, vy.at[half, b], pysend.at[0, i], pyrecv.at[half, b],
               device(x, bpeer(i), z, half))
        for i in range(1, nb)
    ]
    for copy in py:
        copy.start()

    for q, src in later:
        down_part(q, src, block_of(q, src))
    for s in range(2 * nz):
        dg[:, s * feats : s * feats + head] = dgp[s, :, 0:head]
        dg[:, s * feats + head : (s + 1) * feats] = dgp[s, :, LANES : 2 * LANES]
    stores.append(pltpu.make_async_copy(dg, dg_hbm.at[0], store_sem.at[2]))
    stores[-1].start()

    for i in range(1, nb):
        remote(vsum, vy.at[half, bpeer(i)], pysend.at[0, i], pyrecv.at[half, bpeer(i)],
               device(x, bpeer(i), z, half)).wait_recv()
    for i in range(nb):
        remote(vsum, vy.at[1 - half, bpeer(i)], pysend.at[1, i],
               pyrecv.at[1 - half, bpeer(i)], device(x, bpeer(i), z, 1 - half)).wait_recv()
    mine = iota((nb, LANES), 0) == b
    for i in range(nb):
        both = vy[0, i] + vy[1, i]
        usum[i : i + 1, :] = jnp.sum(jnp.where(mine, both, 0.0), axis=0, keepdims=True)
    vx[x] = usum[...]
    px = [
        remote(usum, vx.at[x], pxsend.at[i], pxrecv.at[x], device(xpeer(i), b, z, half))
        for i in farthest(nx)
    ]
    for copy in px:
        copy.start()
    for i in range(1, nx):
        remote(usum, vx.at[xpeer(i)], pxsend.at[i], pxrecv.at[xpeer(i)],
               device(xpeer(i), b, z, half)).wait_recv()
    table = jnp.concatenate(thirds(vx[...].reshape(nx * nb, LANES)), axis=0)
    token_probe = []
    for k in range(2):
        picked = (iota((nx * nb, tokens), 0) == ei[k : k + 1]).astype(F32).astype(BF16)
        found = dot(table, jnp.concatenate([picked] * 3, axis=0), ((0,), (0,)))
        lane = x * cap + si[k : k + 1]
        token_probe.append(
            jnp.sum(jnp.where(iota((LANES, tokens), 0) == lane, found, 0.0), axis=0, keepdims=True)
        )
    slope = (token_probe[0] - token_probe[1]) * share * (1.0 - share)
    rg[0:1] = slope
    rg[1:2] = -slope
    stores.append(pltpu.make_async_copy(rg, rg_hbm, store_sem.at[3]))
    stores[-1].start()

    for copy in xcopies + ycopies + zcopies + pz + py + px:
        copy.wait_send()
    for copy in stores:
        copy.wait()


def write_kernel(dg_in, gg_in, ug_in, rg_in, dg, gg, ug, rg, dg_v, gg_v, ug_v, rg_v, sem_in, sem_out):
    pieces = []
    for source, held, target in (
        (dg_in, dg_v, dg), (gg_in, gg_v, gg), (ug_in, ug_v, ug), (rg_in, rg_v, rg)
    ):
        height = source.shape[-2]
        step = 80 if source is dg_in else height
        for at in range(0, height, step):
            piece = pl.ds(at, min(step, height - at))
            if len(source.shape) == 3:
                pieces.append((source.at[0, piece], held.at[0, piece], target.at[0, piece]))
            else:
                pieces.append((source, held, target))
    reads = [
        pltpu.make_async_copy(source, held, sem_in.at[n])
        for n, (source, held, _) in enumerate(pieces)
    ]
    writes = [
        pltpu.make_async_copy(held, target, sem_out.at[n])
        for n, (_, held, target) in enumerate(pieces)
    ]
    for read in reads:
        read.start()
    for read, write in zip(reads, writes):
        read.wait()
        write.start()
    for write in writes:
        write.wait()


def shards(dims, out_grad, router_logits, expert_ids, slot_ids, down_weight, gate_pre, up_pre):
    nx, ny, nc, nz, cap = dims
    nb = ny * nc
    rows = nx * nb * cap
    tokens, feats = out_grad.shape
    hidden, width = down_weight.shape[1:]
    head = feats - LANES
    packs = LANES // (LANES - head)
    hbm = pl.BlockSpec(memory_space=pl.ANY)
    dma = pltpu.SemaphoreType.DMA
    results = pl.pallas_call(
        functools.partial(kernel, dims),
        out_shape=(
            jax.ShapeDtypeStruct(down_weight.shape, BF16),
            jax.ShapeDtypeStruct((1, hidden, rows), BF16),
            jax.ShapeDtypeStruct((1, hidden, rows), BF16),
            jax.ShapeDtypeStruct((2, tokens), F32),
        ),
        in_specs=[hbm] * 7,
        out_specs=(hbm,) * 4,
        scratch_shapes=[
            pltpu.VMEM((feats, tokens), BF16),
            pltpu.VMEM((2, tokens), F32),
            pltpu.VMEM((2, tokens), jnp.int32),
            pltpu.VMEM((2, tokens), jnp.int32),
            pltpu.VMEM((hidden, width), BF16),
            pltpu.VMEM((hidden, rows), BF16),
            pltpu.VMEM((hidden, rows), BF16),
            pltpu.VMEM((hidden, width), BF16),
            pltpu.VMEM((hidden, rows), BF16),
            pltpu.VMEM((hidden, rows), BF16),
            pltpu.VMEM((2, tokens), F32),
            pltpu.VMEM((rows // 2, rows // 2), BF16),
            pltpu.VMEM((rows, rows), BF16),
            pltpu.VMEM((rows, LANES), BF16),
            pltpu.VMEM((2, 2 * LANES, tokens), BF16),
            pltpu.VMEM((2, 2, nx, nb * cap // 2, LANES), BF16),
            pltpu.VMEM((2, 2, nx, nb * cap // 2, LANES), BF16),
            pltpu.VMEM((2, 2, nb, nx * cap // 2, LANES), BF16),
            pltpu.VMEM((2, 2, 2, nb, nx * cap // 2, LANES), BF16),
            pltpu.VMEM((nz, 2, 2, rows // 2 // packs, packs * head), BF16),
            pltpu.VMEM((nz, 2, 2, rows // 2, LANES), BF16),
            pltpu.VMEM((rows, LANES), BF16),
            pltpu.VMEM((1, rows), F32),
            pltpu.VMEM((2 * nz, hidden, 2 * LANES), BF16),
            pltpu.VMEM((2 * nz, hidden, 2 * LANES), BF16),
            pltpu.VMEM((hidden, rows), F32),
            pltpu.VMEM((hidden, rows), F32),
            pltpu.VMEM((hidden, rows), F32),
            pltpu.VMEM((hidden, rows), F32),
            pltpu.VMEM((hidden, rows), BF16),
            pltpu.VMEM((nz, nb, LANES), F32),
            pltpu.VMEM((2, nb, nb, LANES), F32),
            pltpu.VMEM((nx, nb, LANES), F32),
            pltpu.VMEM((nb, LANES), F32),
            pltpu.VMEM((nb, LANES), F32),
            dma((7,)),
            dma((4,)),
            dma((2, 2, nx)),
            dma((2, 2, nx)),
            dma((2, 2, 2, nb)),
            dma((2, 2, 2, nb)),
            dma((2, 8, nz)),
            dma((8, nz)),
            dma((4,)),
            dma((4,)),
            dma((nz,)),
            dma((nz,)),
            dma((2, nb)),
            dma((2, nb)),
            dma((nx,)),
            dma((nx,)),
        ],
        compiler_params=pltpu.CompilerParams(
            collective_id=0, has_side_effects=True, vmem_limit_bytes=VMEM_BYTES
        ),
    )(
        out_grad.T, router_logits.T, expert_ids.T, slot_ids.T, down_weight,
        gate_pre.transpose(0, 2, 1), up_pre.transpose(0, 2, 1),
    )
    down_grad, gate_grad, up_grad, router_grad = pl.pallas_call(
        write_kernel,
        out_shape=tuple(jax.ShapeDtypeStruct(r.shape, r.dtype) for r in results),
        in_specs=[hbm] * 4,
        out_specs=(hbm,) * 4,
        scratch_shapes=[pltpu.VMEM(r.shape, r.dtype) for r in results] + [dma((5,)), dma((5,))],
        compiler_params=pltpu.CompilerParams(vmem_limit_bytes=VMEM_BYTES),
    )(*results)
    return (
        down_grad, gate_grad.transpose(0, 2, 1), up_grad.transpose(0, 2, 1), router_grad.T
    )


def solution(mesh, dims=(8, 4, 2, 8, 12)):
    placed = (
        P("expert", "tensor"),
        P("expert", None),
        P("expert", None),
        P("expert", None),
        P("expert", "tensor", None),
        P("expert", None, "tensor"),
        P("expert", None, "tensor"),
    )
    return jax.shard_map(
        functools.partial(shards, dims),
        mesh=mesh,
        in_specs=placed,
        out_specs=(
            P("expert", "tensor", None),
            P("expert", None, "tensor"),
            P("expert", None, "tensor"),
            P("expert", None),
        ),
        check_vma=False,
    )
```

```python
import functools

import jax
import jax.numpy as jnp
from jax import lax
from jax.experimental import pallas as pl
from jax.experimental.pallas import tpu as pltpu
from jax.sharding import PartitionSpec as P

MESH = pl.DeviceIdType.MESH
BF16 = jnp.bfloat16
F32 = jnp.float32
LANES = 128
VMEM_BYTES = 62 * 1024 * 1024


def dot(a, b, contract=((1,), (0,))):
    return lax.dot_general(a, b, (contract, ((), ())), preferred_element_type=F32)


def thirds(v):
    first = v.astype(BF16)
    rest = v - first.astype(F32)
    second = rest.astype(BF16)
    return [first, second, (rest - second.astype(F32)).astype(BF16)]


def iota(shape, dim):
    return lax.broadcasted_iota(jnp.int32, shape, dim)


def kernel(
    dims, og_hbm, rl_hbm, ei_hbm, si_hbm, w_hbm, gp_hbm, up_hbm,
    dg_hbm, gg_hbm, ug_hbm, rg_hbm,
    og, rl, ei, si, w, gp, up, dg, gg, ug, rg,
    perm, order, spread, ext, xs, xr, ys, yr, g0, g1, unpacked, sw, wp, dgp, hid, act, f1, f2,
    scaled, vz, vy, vx, vsum, usum, load_sem, store_sem,
    xsend, xrecv, ysend, yrecv, zsend, zrecv, asend, arecv, pzsend, pzrecv, pysend, pyrecv, pxsend, pxrecv,
):
    nx, ny, nc, nz, cap = dims
    nb = ny * nc
    rows = nx * nb * cap
    part_cap = cap // 2
    part_rows = rows // 2
    part_group = nb * part_cap
    feats, tokens = og.shape
    head = feats - LANES
    packs = LANES // (LANES - head)
    packed_rows = part_rows // packs
    hidden = w.shape[0]
    e, t = lax.axis_index("expert"), lax.axis_index("tensor")
    x, b = e // nb, e % nb
    z, half = t // 2, t % 2

    def xpeer(i):
        return lax.rem(x + i, nx)

    def bpeer(i):
        return lax.rem(b + i, nb)

    def zpeer(i):
        return lax.rem(z + i + nz, nz)

    def device(x_, b_, z_, half_):
        return {"expert": x_ * nb + b_, "tensor": z_ * 2 + half_}

    def farthest(n):
        return sorted(range(1, n), key=lambda i: -min(i, n - i))

    def remote(src, dst, send, recv, where):
        return pltpu.make_async_remote_copy(
            src_ref=src, dst_ref=dst, send_sem=send, recv_sem=recv,
            device_id=where, device_id_type=MESH,
        )

    loads = [
        pltpu.make_async_copy(src, dst, load_sem.at[n])
        for n, (src, dst) in enumerate(
            [
                (ei_hbm, ei), (si_hbm, si), (rl_hbm, rl), (og_hbm, og),
                (gp_hbm.at[0], gp), (up_hbm.at[0], up), (w_hbm.at[0], w),
            ]
        )
    ]
    for copy in loads:
        copy.start()

    barrier = pltpu.get_barrier_semaphore()
    peers = [device(xpeer(i), b, z, half) for i in farthest(nx)]
    peers += [device(x, bpeer(i), z, half) for i in range(1, nb)]
    peers += [device(x, bpeer(i), z, 1 - half) for i in range(nb)]
    peers += [device(x, b, zpeer(i), half) for i in range(1, nz)]
    for peer in peers:
        pl.semaphore_signal(barrier, inc=1, device_id=peer, device_id_type=MESH)

    for copy in loads[:4]:
        copy.wait()

    share = jax.nn.sigmoid(rl[0:1, :] - rl[1:2, :])
    combine = [share.astype(BF16).astype(F32), (1.0 - share).astype(BF16).astype(F32)]
    chosen = [[], []]
    for k in range(2):
        ext[k, 0:head] = og[0:head]
        ext[k, LANES : 2 * LANES] = og[head:feats]
        ext[k, head:LANES] = jnp.where(
            iota((LANES - head, tokens), 0) == 0, combine[k], 0.0
        ).astype(BF16)
        for r in range(2):
            place = si[k : k + 1] - r * part_cap
            inside = (place >= 0) & (place < part_cap)
            row = jnp.where(inside, ei[k : k + 1] * part_cap + place, -1)
            chosen[r].append((iota((part_rows, tokens), 0) == row).astype(F32).astype(BF16))

    chunks = [(c, r) for c in range(2) for r in range(2)]
    xcopies = []
    for c, r in chunks:
        cols = slice(c * LANES, (c + 1) * LANES)
        outgoing = dot(chosen[r][0], ext[0, cols], ((1,), (1,)))
        outgoing += dot(chosen[r][1], ext[1, cols], ((1,), (1,)))
        xs[c, r] = outgoing.astype(BF16).reshape(nx, part_group, LANES)
        if (c, r) == (0, 0):
            pl.semaphore_wait(barrier, len(peers))
        for i in farthest(nx):
            copy = remote(xs.at[c, r, xpeer(i)], xr.at[c, r, x], xsend.at[c, r, i],
                          xrecv.at[c, r, x], device(xpeer(i), b, z, half))
            copy.start()
            xcopies.append(copy)

    i_row = iota((part_rows, 1), 0)
    major = i_row // (nx * part_cap)
    rest = i_row - major * (nx * part_cap)
    minor = rest // part_cap
    source = minor * part_group + major * part_cap + (rest - minor * part_cap)
    perm[...] = (iota((part_rows, part_rows), 1) == source).astype(F32).astype(BF16)

    n_lane = iota((1, rows), 1)
    n_part = n_lane // part_rows
    n_rest = n_lane - n_part * part_rows
    n_source = n_rest // part_cap
    n_slot = n_rest - n_source * part_cap
    origin = n_source * cap + n_part * part_cap + n_slot
    order[...] = (iota((rows, rows), 0) == origin).astype(F32).astype(BF16)

    i_row = iota((rows, 1), 0)
    i_part = i_row // part_rows
    i_rest = i_row - i_part * part_rows
    i_source = i_rest // part_cap
    i_lane = (i_source // nb) * cap + i_part * part_cap + (i_rest - i_source * part_cap)
    spread[...] = (iota((rows, LANES), 1) == i_lane).astype(F32).astype(BF16)

    for copy in loads[4:]:
        copy.wait()
    for s in range(2 * nz):
        wp[s, :, 0:head] = w[:, s * feats : s * feats + head]
        wp[s, :, head:LANES] = jnp.zeros((hidden, LANES - head), BF16)
        wp[s, :, LANES : 2 * LANES] = w[:, s * feats + head : (s + 1) * feats]
    gate = dot(gp[...], order[...])
    upf = dot(up[...], order[...])
    sigma = jax.nn.sigmoid(gate)
    silu = gate * sigma
    act[...] = silu * upf
    f1[...] = upf * (sigma * (1.0 + gate * (1.0 - sigma)))
    f2[...] = silu
    hid[...] = jnp.zeros_like(hid)
    unpacked[...] = jnp.zeros_like(unpacked)

    ycopies = []

    def ysend_start(c, r, h):
        for i in range(1 - h, nb):
            copy = remote(ys.at[c, r, bpeer(i)], yr.at[h, c, r, b], ysend.at[h, c, r, i],
                          yrecv.at[h, c, r, b],
                          device(x, bpeer(i), z, half if h == 0 else 1 - half))
            copy.start()
            ycopies.append(copy)

    for c, r in chunks:
        xr[c, r, x] = xs[c, r, x]
        for i in range(1, nx):
            remote(xs.at[c, r, x], xr.at[c, r, xpeer(i)], xsend.at[c, r, i],
                   xrecv.at[c, r, xpeer(i)], device(xpeer(i), b, z, half)).wait_recv()
        turned = dot(perm[...], xr[c, r].reshape(part_rows, LANES)).astype(BF16)
        ys[c, r] = turned.reshape(nb, nx * part_cap, LANES)
        yr[0, c, r, b] = ys[c, r, b]
        ysend_start(c, r, 0)

    longer, shorter = nz // 2, nz - 1 - nz // 2
    hops = [(longer, shorter), (shorter, longer), (shorter, shorter), (shorter, shorter)]
    zcopies = []

    def zref(q, src):
        h, c, r = q // 4, q // 2 % 2, q % 2
        return (g1 if c else g0).at[src, h, r]

    def zsend_start(q, src, way):
        to = zpeer(1) if way == 0 else zpeer(-1)
        copy = remote(zref(q, src), zref(q, src), zsend.at[way, q, src], zrecv.at[q, src],
                      device(x, b, to, half))
        copy.start()
        zcopies.append(copy)

    def zwait(q, src):
        remote(zref(q, src), zref(q, src), zsend.at[0, q, src], zrecv.at[q, src],
               device(x, b, zpeer(1), half)).wait_recv()

    def across(q, src):
        return remote(zref(q, src), zref(q + 4, src), asend.at[q], arecv.at[q],
                      device(x, b, z, 1 - half))

    def block_of(q, src):
        h, c = q // 4, q // 2 % 2
        if c == 1:
            return g1[src, h].reshape(rows, LANES)
        for r in range(2):
            for n in range(packs):
                at = r * part_rows + n * packed_rows
                unpacked[at : at + packed_rows, 0:head] = g0[
                    src, h, r, :, n * head : (n + 1) * head
                ]
        return unpacked[...]

    def place_of(q, src):
        h, c = q // 4, q // 2 % 2
        return src * 2 + (half if h == 0 else 1 - half), slice(c * LANES, (c + 1) * LANES)

    def hidden_part(q, src, block):
        shard, cols = place_of(q, src)
        hid[...] += dot(wp[shard, :, cols], block, ((1,), (1,)))

    def down_part(q, src, block):
        shard, cols = place_of(q, src)
        dgp[shard, :, cols] = dot(scaled[...], block).astype(BF16)

    def own(q):
        h, c, r = q // 4, q // 2 % 2, q % 2
        for i in range(1 - h, nb):
            remote(ys.at[c, r, b], yr.at[h, c, r, bpeer(i)], ysend.at[h, c, r, i],
                   yrecv.at[h, c, r, bpeer(i)], device(x, bpeer(i), z, half)).wait_recv()
        canon = dot(perm[...], yr[h, c, r].reshape(part_rows, LANES),
                    ((0,), (0,)) if nx != nb else ((1,), (0,))).astype(BF16)
        if c == 0:
            for n in range(packs):
                g0[z, h, r, :, n * head : (n + 1) * head] = canon[
                    n * packed_rows : (n + 1) * packed_rows, 0:head
                ]
        else:
            g1[z, h, r] = canon
        zsend_start(q, z, 0)
        zsend_start(q, z, 1)
        if q < 2:
            pick = (iota((8, LANES), 1) == head).astype(F32).astype(BF16)
            sw[:, q * part_rows : (q + 1) * part_rows] = dot(pick, canon, ((1,), (1,)))[0:1]

    steps = [(0, s) for s in range(nz // 2)] + [(1, 0), (0, nz // 2)]
    steps += [(1, s) for s in range(1, nz // 2 + 1)]
    later = []
    for n, (h, s) in enumerate(steps):
        done = []
        if s == 0:
            for q in range(4 * h, 4 * h + 4):
                own(q)
                if q % 2 == 1:
                    done.append((q, z))
            if h == 0:
                scaled[...] = (sw[...] * act[...]).astype(BF16)
                for c, r in chunks:
                    ysend_start(c, r, 1)
        else:
            for turn in range(2):
                for r in range(2):
                    for way in range(2):
                        c = turn if hops[2 * h][way] >= hops[2 * h + 1][way] else 1 - turn
                        q = 4 * h + 2 * c + r
                        if s <= hops[2 * h + c][way]:
                            src = zpeer(-s) if way == 0 else zpeer(s)
                            zwait(q, src)
                            if s < hops[2 * h + c][way]:
                                zsend_start(q, src, way)
                            if h == 0 and s == longer:
                                copy = across(q, src)
                                copy.start()
                                zcopies.append(copy)
                            if r == 1:
                                done.append((q, src))
            if h == 1 and s == longer:
                for q in range(4):
                    across(q, zpeer(longer)).wait_recv()
                done += [(5, zpeer(longer)), (7, zpeer(longer))]
        for q, src in done:
            block = block_of(q, src)
            hidden_part(q, src, block)
            if n < len(steps) - 2:
                down_part(q, src, block)
            else:
                later.append((q, src))

    probe = jnp.sum(hid[...] * act[...], axis=0, keepdims=True)
    parted = jnp.where(iota((nb, rows), 0) == n_source - (n_source // nb) * nb, probe, 0.0)
    parts = dot(jnp.concatenate(thirds(parted), axis=0), spread[...])
    vz[z] = parts[0:nb] + parts[nb : 2 * nb] + parts[2 * nb : 3 * nb]
    pz = [
        remote(vz.at[z], vz.at[z], pzsend.at[i], pzrecv.at[z], device(x, b, zpeer(i), half))
        for i in farthest(nz)
    ]
    for copy in pz:
        copy.start()

    gg[...] = dot((hid[...] * (sw[...] * f1[...])).astype(BF16), order[...], ((1,), (1,))).astype(BF16)
    ug[...] = dot((hid[...] * (sw[...] * f2[...])).astype(BF16), order[...], ((1,), (1,))).astype(BF16)
    stores = [
        pltpu.make_async_copy(gg, gg_hbm.at[0], store_sem.at[0]),
        pltpu.make_async_copy(ug, ug_hbm.at[0], store_sem.at[1]),
    ]
    for copy in stores:
        copy.start()

    for i in range(1, nz):
        remote(vz.at[z], vz.at[zpeer(i)], pzsend.at[i], pzrecv.at[zpeer(i)],
               device(x, b, zpeer(i), half)).wait_recv()
    vsum[...] = jnp.sum(vz[...], axis=0)
    vy[half, b] = vsum[...]
    py = [
        remote(vsum, vy.at[half, b], pysend.at[1, i], pyrecv.at[half, b],
               device(x, bpeer(i), z, 1 - half))
        for i in range(nb)
    ]
    py += [
        remote(vsum, vy.at[half, b], pysend.at[0, i], pyrecv.at[half, b],
               device(x, bpeer(i), z, half))
        for i in range(1, nb)
    ]
    for copy in py:
        copy.start()

    for q, src in later:
        down_part(q, src, block_of(q, src))
    for s in range(2 * nz):
        dg[:, s * feats : s * feats + head] = dgp[s, :, 0:head]
        dg[:, s * feats + head : (s + 1) * feats] = dgp[s, :, LANES : 2 * LANES]
    stores.append(pltpu.make_async_copy(dg, dg_hbm.at[0], store_sem.at[2]))
    stores[-1].start()

    for i in range(1, nb):
        remote(vsum, vy.at[half, bpeer(i)], pysend.at[0, i], pyrecv.at[half, bpeer(i)],
               device(x, bpeer(i), z, half)).wait_recv()
    for i in range(nb):
        remote(vsum, vy.at[1 - half, bpeer(i)], pysend.at[1, i],
               pyrecv.at[1 - half, bpeer(i)], device(x, bpeer(i), z, 1 - half)).wait_recv()
    mine = iota((nb, LANES), 0) == b
    for i in range(nb):
        both = vy[0, i] + vy[1, i]
        usum[i : i + 1, :] = jnp.sum(jnp.where(mine, both, 0.0), axis=0, keepdims=True)
    vx[x] = usum[...]
    px = [
        remote(usum, vx.at[x], pxsend.at[i], pxrecv.at[x], device(xpeer(i), b, z, half))
        for i in farthest(nx)
    ]
    for copy in px:
        copy.start()
    for i in range(1, nx):
        remote(usum, vx.at[xpeer(i)], pxsend.at[i], pxrecv.at[xpeer(i)],
               device(xpeer(i), b, z, half)).wait_recv()
    table = jnp.concatenate(thirds(vx[...].reshape(nx * nb, LANES)), axis=0)
    token_probe = []
    for k in range(2):
        picked = (iota((nx * nb, tokens), 0) == ei[k : k + 1]).astype(F32).astype(BF16)
        found = dot(table, jnp.concatenate([picked] * 3, axis=0), ((0,), (0,)))
        lane = x * cap + si[k : k + 1]
        token_probe.append(
            jnp.sum(jnp.where(iota((LANES, tokens), 0) == lane, found, 0.0), axis=0, keepdims=True)
        )
    slope = (token_probe[0] - token_probe[1]) * share * (1.0 - share)
    rg[0:1] = slope
    rg[1:2] = -slope
    stores.append(pltpu.make_async_copy(rg, rg_hbm, store_sem.at[3]))
    stores[-1].start()

    for copy in xcopies + ycopies + zcopies + pz + py + px:
        copy.wait_send()
    for copy in stores:
        copy.wait()


def write_kernel(dg_in, gg_in, ug_in, rg_in, dg, gg, ug, rg, dg_v, gg_v, ug_v, rg_v, sem_in, sem_out):
    pieces = []
    for source, held, target in (
        (dg_in, dg_v, dg), (gg_in, gg_v, gg), (ug_in, ug_v, ug), (rg_in, rg_v, rg)
    ):
        height = source.shape[-2]
        step = height
        for at in range(0, height, step):
            piece = pl.ds(at, min(step, height - at))
            if len(source.shape) == 3:
                pieces.append((source.at[0, piece], held.at[0, piece], target.at[0, piece]))
            else:
                pieces.append((source, held, target))
    reads = [
        pltpu.make_async_copy(source, held, sem_in.at[n])
        for n, (source, held, _) in enumerate(pieces)
    ]
    writes = [
        pltpu.make_async_copy(held, target, sem_out.at[n])
        for n, (_, held, target) in enumerate(pieces)
    ]
    for read in reads:
        read.start()
    for read, write in zip(reads, writes):
        read.wait()
        write.start()
    for write in writes:
        write.wait()


def shards(dims, out_grad, router_logits, expert_ids, slot_ids, down_weight, gate_pre, up_pre):
    nx, ny, nc, nz, cap = dims
    nb = ny * nc
    rows = nx * nb * cap
    tokens, feats = out_grad.shape
    hidden, width = down_weight.shape[1:]
    head = feats - LANES
    packs = LANES // (LANES - head)
    hbm = pl.BlockSpec(memory_space=pl.ANY)
    dma = pltpu.SemaphoreType.DMA
    results = pl.pallas_call(
        functools.partial(kernel, dims),
        out_shape=(
            jax.ShapeDtypeStruct(down_weight.shape, BF16),
            jax.ShapeDtypeStruct((1, hidden, rows), BF16),
            jax.ShapeDtypeStruct((1, hidden, rows), BF16),
            jax.ShapeDtypeStruct((2, tokens), F32),
        ),
        in_specs=[hbm] * 7,
        out_specs=(hbm,) * 4,
        scratch_shapes=[
            pltpu.VMEM((feats, tokens), BF16),
            pltpu.VMEM((2, tokens), F32),
            pltpu.VMEM((2, tokens), jnp.int32),
            pltpu.VMEM((2, tokens), jnp.int32),
            pltpu.VMEM((hidden, width), BF16),
            pltpu.VMEM((hidden, rows), BF16),
            pltpu.VMEM((hidden, rows), BF16),
            pltpu.VMEM((hidden, width), BF16),
            pltpu.VMEM((hidden, rows), BF16),
            pltpu.VMEM((hidden, rows), BF16),
            pltpu.VMEM((2, tokens), F32),
            pltpu.VMEM((rows // 2, rows // 2), BF16),
            pltpu.VMEM((rows, rows), BF16),
            pltpu.VMEM((rows, LANES), BF16),
            pltpu.VMEM((2, 2 * LANES, tokens), BF16),
            pltpu.VMEM((2, 2, nx, nb * cap // 2, LANES), BF16),
            pltpu.VMEM((2, 2, nx, nb * cap // 2, LANES), BF16),
            pltpu.VMEM((2, 2, nb, nx * cap // 2, LANES), BF16),
            pltpu.VMEM((2, 2, 2, nb, nx * cap // 2, LANES), BF16),
            pltpu.VMEM((nz, 2, 2, rows // 2 // packs, packs * head), BF16),
            pltpu.VMEM((nz, 2, 2, rows // 2, LANES), BF16),
            pltpu.VMEM((rows, LANES), BF16),
            pltpu.VMEM((1, rows), F32),
            pltpu.VMEM((2 * nz, hidden, 2 * LANES), BF16),
            pltpu.VMEM((2 * nz, hidden, 2 * LANES), BF16),
            pltpu.VMEM((hidden, rows), F32),
            pltpu.VMEM((hidden, rows), F32),
            pltpu.VMEM((hidden, rows), F32),
            pltpu.VMEM((hidden, rows), F32),
            pltpu.VMEM((hidden, rows), BF16),
            pltpu.VMEM((nz, nb, LANES), F32),
            pltpu.VMEM((2, nb, nb, LANES), F32),
            pltpu.VMEM((nx, nb, LANES), F32),
            pltpu.VMEM((nb, LANES), F32),
            pltpu.VMEM((nb, LANES), F32),
            dma((7,)),
            dma((4,)),
            dma((2, 2, nx)),
            dma((2, 2, nx)),
            dma((2, 2, 2, nb)),
            dma((2, 2, 2, nb)),
            dma((2, 8, nz)),
            dma((8, nz)),
            dma((4,)),
            dma((4,)),
            dma((nz,)),
            dma((nz,)),
            dma((2, nb)),
            dma((2, nb)),
            dma((nx,)),
            dma((nx,)),
        ],
        compiler_params=pltpu.CompilerParams(
            collective_id=0, has_side_effects=True, vmem_limit_bytes=VMEM_BYTES
        ),
    )(
        out_grad.T, router_logits.T, expert_ids.T, slot_ids.T, down_weight,
        gate_pre.transpose(0, 2, 1), up_pre.transpose(0, 2, 1),
    )
    down_grad, gate_grad, up_grad, router_grad = pl.pallas_call(
        write_kernel,
        out_shape=tuple(jax.ShapeDtypeStruct(r.shape, r.dtype) for r in results),
        in_specs=[hbm] * 4,
        out_specs=(hbm,) * 4,
        scratch_shapes=[pltpu.VMEM(r.shape, r.dtype) for r in results] + [dma((5,)), dma((5,))],
        compiler_params=pltpu.CompilerParams(vmem_limit_bytes=VMEM_BYTES),
    )(*results)
    return (
        down_grad, gate_grad.transpose(0, 2, 1), up_grad.transpose(0, 2, 1), router_grad.T
    )


def solution(mesh, dims=(8, 4, 2, 8, 12)):
    placed = (
        P("expert", "tensor"),
        P("expert", None),
        P("expert", None),
        P("expert", None),
        P("expert", "tensor", None),
        P("expert", None, "tensor"),
        P("expert", None, "tensor"),
    )
    return jax.shard_map(
        functools.partial(shards, dims),
        mesh=mesh,
        in_specs=placed,
        out_specs=(
            P("expert", "tensor", None),
            P("expert", None, "tensor"),
            P("expert", None, "tensor"),
            P("expert", None),
        ),
        check_vma=False,
    )
```
